512 devices in a mesh: row: 32 (over y, x, core), col: 16 (over z).
Axes of the slice: x: 4, y: 4, z: 16, core: 2. Of those that a mesh axis runs over, the one named last changes fastest.
Arguments:
- covariance: float32 [8192, 8192], P('row', 'col'), may hold values from -4 to 60, as said below
- observations: float32 [64, 8192], P(None, 'row'), may hold values from -6 to 6
Outputs:
- factored: float32 [8192, 8192], P('row', 'col')
- solved: float32 [64, 8192], P(None, 'row')
- site_terms: float32 [64], replicated
The draws below stay inside these ranges and needn't reach their ends.
Inputs may be any that keep to these rules, and one draw needn't show every extreme that they name: `covariance`: symmetric and positive definite.
All inputs are finite; a program needn't handle non-finite values.
Results may differ from the reference program's by a relative error of at most 0.0001.
Values sent between devices are 32-bit elements; how exact they have to be, the bound alone decides.
No kernel may reach another device: no remote copies, remote signals or barrier semaphores. Data moves between devices by JAX's collectives and lax.ppermute only.
A program may use at most 64 MiB of HBM per device.

```python
import math
import jax
import jax.numpy as jnp
from jax import lax

TILE = 256
NRHS = 64
M = 8192


def draw_covariance(key, part):
    key = jax.random.fold_in(key, 7)
    key_place, key_scale, key_jitter = jax.random.split(key, 3)
    places = jax.random.uniform(key_place, (M, 2), jnp.float32)
    spread = math.log(3.2)
    jitter = jnp.clip(jax.random.normal(key_jitter, (M, M), jnp.float32), -4.0, 4.0)
    scales = jnp.exp(jax.random.uniform(key_scale, (M,), jnp.float32, 0.0, spread))
    delta_x = places[:, 0][:, None] - places[:, 0][None, :]
    delta_y = places[:, 1][:, None] - places[:, 1][None, :]
    spacing = jnp.sqrt(delta_x * delta_x + delta_y * delta_y)
    kernel = jnp.exp(-spacing / 0.02)
    symmetric = (jitter + jitter.T) * (0.35 / math.sqrt(M))
    matern_part = kernel + symmetric + 2.5 * jnp.eye(M, dtype=jnp.float32)
    return matern_part * scales[:, None] * scales[None, :]


def level_of(key, extent, cuts, low, high):
    def one(position, parts):
        heights = jax.random.uniform(jax.random.fold_in(jax.random.fold_in(key, 6), position), (parts,), jnp.float32, low / len(cuts), high / len(cuts))
        return jnp.repeat(jnp.exp(heights), extent[position] // parts).reshape((-1,) + (1,) * (len(extent) - position - 1))

    gain = one(*cuts[0])
    for cut in cuts[1:]:
        gain = gain * one(*cut)
    return gain


def gaussian(rng, shape, width, reach, cuts=(), kind=jnp.bfloat16):
    level = level_of(rng, shape, cuts, -0.22, 0.18) if cuts else 1.0
    result = jax.random.normal(rng, shape, jnp.float32) * width * level
    return jnp.minimum(jnp.maximum(result, -reach), reach).astype(kind)


def setup_inputs(seed: int = 0) -> dict:
    streams_of = jax.random.split(jax.random.key(seed), 3)
    return {
        "covariance": draw_covariance(jax.random.fold_in(streams_of[2], 71), 0),
        "observations": gaussian(streams_of[1], (NRHS, M), 1.0, 6.0, ((1, 32),), jnp.float32),
    }


def reference(covariance, observations):
    current = covariance
    targets = observations
    log_total = jnp.zeros((), jnp.float32)
    quadratic = jnp.zeros((NRHS,), jnp.float32)
    for section in range(2):
        start_col = section * TILE
        end_col = start_col + TILE
        chol_factor = jnp.linalg.cholesky(current[start_col:end_col, start_col:end_col])
        below_rows = jax.scipy.linalg.solve_triangular(chol_factor, current[end_col:, start_col:end_col].T, lower=True).T
        solved_obs = jax.scipy.linalg.solve_triangular(chol_factor, targets[:, start_col:end_col].T, lower=True)
        reduced = targets[:, end_col:] - jnp.dot(below_rows, solved_obs, precision=lax.Precision.HIGHEST).T
        targets = targets.at[:, end_col:].set(reduced)
        targets = targets.at[:, start_col:end_col].set(solved_obs.T)
        trailing = current[end_col:, end_col:] - jnp.dot(below_rows, below_rows.T, precision=lax.Precision.HIGHEST)
        current = current.at[end_col:, end_col:].set(trailing)
        current = current.at[start_col:end_col, start_col:end_col].set(chol_factor)
        current = current.at[end_col:, start_col:end_col].set(below_rows)
        current = current.at[start_col:end_col, end_col:].set(jnp.zeros((TILE, M - end_col), current.dtype))
        log_total = log_total + 2.0 * jnp.sum(jnp.log(jnp.diagonal(chol_factor)))
        quadratic = quadratic + jnp.sum(solved_obs * solved_obs, axis=0)
    site_terms = -(quadratic + log_total) / (4.0 * TILE)
    return (current, targets, site_terms)
```

```python
import jax
import jax.numpy as jnp
from jax import lax
from jax.sharding import PartitionSpec as P

HI = lax.Precision.HIGHEST


def dot(a, b):
    return jnp.dot(a, b, precision=HI)


def tree_step(value, hop, extent, position):
    pairs = [(z, z + hop) for z in range(0, extent, 2 * hop)]
    moved = lax.ppermute(value, "col", pairs)
    return jnp.where(position % (2 * hop) == hop, moved, value)


def factor(block):
    chol = jnp.linalg.cholesky(block)
    inv = jax.scipy.linalg.solve_triangular(
        chol, jnp.eye(block.shape[0], dtype=block.dtype), lower=True
    )
    return chol, inv


def shards(covariance, observations):
    tile, wide = covariance.shape
    nrhs = observations.shape[0]
    rows = lax.axis_size("row")
    cols = lax.axis_size("col")
    row = lax.axis_index("row")
    col = lax.axis_index("col")
    part = tile // rows

    with jax.named_scope("scatter"):
        obs_parts = observations.reshape(rows, part // 2, -1)
        lanes = obs_parts.shape[2]
        obs_parts = jnp.pad(obs_parts, ((0, 0), (0, part - part // 2), (0, 0)))
        sent = jnp.concatenate([covariance.reshape(rows, part, wide), obs_parts], axis=2)
        got = lax.all_to_all(sent, "row", split_axis=0, concat_axis=0, tiled=True)
        first, second = got[0], got[1]

    with jax.named_scope("columns"):
        col_piece = jnp.concatenate([first[:, :wide], second[:, :wide]], axis=0)
        col_all = lax.all_gather(col_piece, "row", axis=0, tiled=False)
        col0 = col_all[:, :part].reshape(tile, wide)
        col1 = col_all[:, part:].reshape(tile, wide)

    hops = []
    hop = cols // 2
    while hop >= 1:
        hops.append(hop)
        hop //= 2

    with jax.named_scope("diag"):
        diag_piece = jnp.concatenate([first[:, :tile], second[:, :wide]], axis=1)
        for hop in hops:
            diag_piece = tree_step(diag_piece, hop, cols, col)
        obs_piece = jnp.concatenate([first[: part // 2, wide:], second[: part // 2, wide:]], axis=0)
        piece = jnp.concatenate([diag_piece, obs_piece], axis=1)
        spread = jnp.broadcast_to(piece[None], (rows,) + piece.shape)
        whole = lax.all_to_all(spread, "row", split_axis=0, concat_axis=0, tiled=True)
        diag00 = whole[:, :, :tile].reshape(tile, tile)
        diag10 = whole[:, :, tile : 2 * tile].reshape(tile, tile)
        diag11 = whole[:, :, 2 * tile : 3 * tile].reshape(tile, tile)
        obs0 = whole[:, : part // 2, 3 * tile :].reshape(nrhs, tile)
        obs1 = whole[:, part // 2 :, 3 * tile :].reshape(nrhs, tile)

    with jax.named_scope("rowpanel"):
        panel = covariance
        for hop in hops:
            panel = tree_step(panel, hop, cols, col)
        row0, row1 = panel[:, :tile], panel[:, tile:]

    chol0, inv0 = factor(diag00)
    low = dot(diag10, inv0.T)
    chol1, inv1 = factor(diag11 - dot(low, low.T))

    with jax.named_scope("solve"):
        x0 = dot(row0, inv0.T)
        x1 = dot(row1 - dot(x0, low.T), inv1.T)
        y0 = dot(inv0, col0)
        y1 = dot(inv1, col1 - dot(low, y0))
        z0 = dot(obs0, inv0.T)
        z1 = dot(obs1 - dot(z0, low.T), inv1.T)

    with jax.named_scope("update"):
        trail = covariance - dot(x0, y0) - dot(x1, y1)
        is0, is1 = row == 0, row == 1
        left = jnp.where(is0, chol0, jnp.where(is1, low, x0))
        right = jnp.where(is0, 0.0, jnp.where(is1, chol1, x1))
        other = jnp.where(row <= 1, 0.0, trail)
        factored = jnp.where(col == 0, jnp.concatenate([left, right], axis=1), other)
        reduced = observations - dot(z0, x0.T) - dot(z1, x1.T)
        solved = jnp.where(is0, z0, jnp.where(is1, z1, reduced))

    with jax.named_scope("terms"):
        logdet = 2.0 * (jnp.sum(jnp.log(jnp.diagonal(chol0))) + jnp.sum(jnp.log(jnp.diagonal(chol1))))
        quad = jnp.sum(z0 * z0, axis=1) + jnp.sum(z1 * z1, axis=1)
        site_terms = -(quad + logdet) / (4.0 * tile)
    return factored, solved, site_terms


def solution(mesh):
    in_specs = (P("row", "col"), P(None, "row"))
    out_specs = (P("row", "col"), P(None, "row"), P())
    return jax.shard_map(shards, mesh=mesh, in_specs=in_specs, out_specs=out_specs, check_vma=False)
```

```python
import jax
import jax.numpy as jnp
from jax import lax
from jax.experimental import pallas as pl
from jax.experimental.pallas import tpu as pltpu
from jax.sharding import PartitionSpec as P

HI = lax.Precision.HIGHEST


def dot(a, b):
    return jnp.dot(a, b, precision=HI)


def tree_step(value, hop, extent, position):
    pairs = [(z, z + hop) for z in range(0, extent, 2 * hop)]
    moved = lax.ppermute(value, "col", pairs)
    return jnp.where(position % (2 * hop) == hop, moved, value)


SUB = 8
LANES = 128


def factor_tile(blocks):
    shape = (SUB, LANES)
    lane = lax.broadcasted_iota(jnp.int32, shape, 1)
    sub = lax.broadcasted_iota(jnp.int32, shape, 0)
    count = len(blocks)
    blocks = list(blocks)
    upper, inverse = [], []
    for b in range(count):
        base = b * SUB
        here = blocks[b]
        across = [jnp.broadcast_to(here[:, base + k : base + k + 1], shape) for k in range(SUB)]
        rows = [jnp.broadcast_to(here[k : k + 1, :], shape) for k in range(SUB)]
        s = {}
        for k in range(SUB):
            for i in range(k, SUB):
                s[i, k] = jnp.broadcast_to(across[k][i : i + 1, :], shape)
        rinv, low, u, w = [], {}, [], []
        for k in range(SUB):
            rinv.append(lax.rsqrt(s[k, k]))
            for i in range(k + 1, SUB):
                low[i, k] = s[i, k] * rinv[k]
            for j in range(k + 1, SUB):
                for i in range(j, SUB):
                    s[i, j] = s[i, j] - low[i, k] * low[j, k]
            uk = rows[k]
            wk = jnp.where(lane < base, rows[k], jnp.where(lane == base + k, 1.0, 0.0))
            for m in range(k):
                uk = uk - low[k, m] * u[m]
                wk = wk - low[k, m] * w[m]
            u.append(uk * rinv[k])
            w.append(wk * rinv[k])
        u_block, w_block = u[0], w[0]
        for k in range(1, SUB):
            u_block = jnp.where(sub == k, u[k], u_block)
            w_block = jnp.where(sub == k, w[k], w_block)
        upper.append(jnp.where(lane >= sub + base, u_block, 0.0))
        inverse.append(w_block)
        if b + 1 == count:
            break
        q = [None] * SUB
        for k in reversed(range(SUB)):
            v = jnp.where(lane < base + SUB, w[k], u[k])
            for m in range(k + 1, SUB):
                v = v - low[m, k] * q[m]
            q[k] = v * rinv[k]
        keep = (lane < base) | (lane >= base + SUB)
        for i in range(b + 1, count):
            old = blocks[i]
            terms = [
                jnp.broadcast_to(old[:, base + k : base + k + 1], shape) * q[k] for k in range(SUB)
            ]
            while len(terms) > 1:
                terms = [terms[t] + terms[t + 1] for t in range(0, len(terms), 2)]
            blocks[i] = jnp.where(keep, old, 0.0) - terms[0]
    return upper, inverse


def factor_kernel(d00_ref, d1_ref, low_ref, inv_ref, work):
    tile = d00_ref.shape[0]
    size = 2 * tile
    work[:tile, :tile] = d00_ref[...]
    work[tile:, :] = d1_ref[...]
    work[:tile, tile:] = d1_ref[:, :tile].T
    row_id = lax.broadcasted_iota(jnp.int32, (size, LANES), 0)
    col_id = lax.broadcasted_iota(jnp.int32, (LANES, size), 1)

    def step(t, carry):
        base = pl.multiple_of(t * LANES, LANES)
        tile_rows = pl.ds(base, LANES)
        here = [work[pl.ds(base + SUB * i, SUB), tile_rows] for i in range(LANES // SUB)]
        up, inv = factor_tile(here)
        up = jnp.concatenate(up, axis=0)
        inv = jnp.concatenate(inv, axis=0)
        across = jnp.dot(inv, work[tile_rows, :], precision=HI, preferred_element_type=jnp.float32)
        below = lax.dot_general(
            work[:, tile_rows], inv, (((1,), (1,)), ((), ())), precision=HI,
            preferred_element_type=jnp.float32,
        )
        below = jnp.where(row_id >= base + LANES, below, 0.0)
        low_ref[:, tile_rows] = below
        low_ref[tile_rows, tile_rows] = up.T
        inv_ref[tile_rows, :] = jnp.where(col_id < base, across, 0.0)
        inv_ref[tile_rows, tile_rows] = inv
        work[tile_rows, :] = across
        work[tile_rows, tile_rows] = inv
        across = work[tile_rows, :]
        work[:, tile_rows] = jnp.zeros((size, LANES), jnp.float32)
        work[...] = work[...] - jnp.dot(
            below, across, precision=HI, preferred_element_type=jnp.float32
        )
        return carry

    lax.fori_loop(0, size // LANES, step, 0)


def factor(d00, d1):
    tile = d00.shape[0]
    size = 2 * tile
    return pl.pallas_call(
        factor_kernel,
        out_shape=[jax.ShapeDtypeStruct((size, size), jnp.float32)] * 2,
        in_specs=[pl.BlockSpec(memory_space=pltpu.VMEM)] * 2,
        out_specs=[pl.BlockSpec(memory_space=pltpu.VMEM)] * 2,
        scratch_shapes=[pltpu.VMEM((size, size), jnp.float32)],
        compiler_params=pltpu.CompilerParams(vmem_limit_bytes=32 * 1024 * 1024),
        cost_estimate=pl.CostEstimate(flops=2 * size**3, bytes_accessed=16 * size * size, transcendentals=size),
        name="factor",
    )(d00, d1)


def shards(covariance, observations):
    tile, wide = covariance.shape
    nrhs = observations.shape[0]
    rows = lax.axis_size("row")
    cols = lax.axis_size("col")
    row = lax.axis_index("row")
    col = lax.axis_index("col")
    part = tile // rows

    with jax.named_scope("scatter"):
        obs_parts = observations.reshape(rows, part // 2, -1)
        lanes = obs_parts.shape[2]
        obs_parts = jnp.pad(obs_parts, ((0, 0), (0, part - part // 2), (0, 0)))
        sent = jnp.concatenate([covariance.reshape(rows, part, wide), obs_parts], axis=2)
        got = lax.all_to_all(sent, "row", split_axis=0, concat_axis=0, tiled=True)
        first, second = got[0], got[1]

    with jax.named_scope("columns"):
        col_piece = jnp.concatenate([first[:, :wide], second[:, :wide]], axis=0)
        col_all = lax.all_gather(col_piece, "row", axis=0, tiled=False)
        columns = jnp.concatenate(
            [col_all[:, :part].reshape(tile, wide), col_all[:, part:].reshape(tile, wide)], axis=0
        )

    hops = []
    hop = cols // 2
    while hop >= 1:
        hops.append(hop)
        hop //= 2

    with jax.named_scope("diag"):
        diag_piece = jnp.concatenate([first[:, :tile], second[:, :wide]], axis=1)
        for hop in hops:
            diag_piece = tree_step(diag_piece, hop, cols, col)
        obs_piece = jnp.concatenate([first[: part // 2, wide:], second[: part // 2, wide:]], axis=0)
        piece = jnp.concatenate([diag_piece, obs_piece], axis=1)
        spread = jnp.broadcast_to(piece[None], (rows,) + piece.shape)
        whole = lax.all_to_all(spread, "row", split_axis=0, concat_axis=0, tiled=True)
        diag0 = whole[:, :, :tile].reshape(tile, tile)
        diag1 = whole[:, :, tile : 3 * tile].reshape(tile, wide)
        obs0 = whole[:, : part // 2, 3 * tile :].reshape(nrhs, tile)
        obs1 = whole[:, part // 2 :, 3 * tile :].reshape(nrhs, tile)
        obs_both = jnp.concatenate([obs0, obs1], axis=1)

    with jax.named_scope("rowpanel"):
        panel = covariance
        for hop in hops:
            panel = tree_step(panel, hop, cols, col)

    low, inv = factor(diag0, diag1)

    with jax.named_scope("solve"):
        x = dot(panel, inv.T)
        y = dot(inv, columns)
        z = dot(obs_both, inv.T)

    with jax.named_scope("update"):
        trail = covariance - dot(x, y)
        first_rows = jnp.where(row == 0, low[:tile], low[tile:])
        edge = jnp.where(row <= 1, first_rows, x)
        other = jnp.where(row <= 1, 0.0, trail)
        factored = jnp.where(col == 0, edge, other)
        reduced = observations - dot(z, x.T)
        solved = jnp.where(row == 0, z[:, :tile], jnp.where(row == 1, z[:, tile:], reduced))

    with jax.named_scope("terms"):
        logdet = 2.0 * jnp.sum(jnp.log(jnp.diagonal(low)))
        quad = jnp.sum(z * z, axis=1)
        site_terms = -(quad + logdet) / (4.0 * tile)
    return factored, solved, site_terms


def solution(mesh):
    in_specs = (P("row", "col"), P(None, "row"))
    out_specs = (P("row", "col"), P(None, "row"), P())
    return jax.shard_map(shards, mesh=mesh, in_specs=in_specs, out_specs=out_specs, check_vma=False)
```

```python
import jax
import jax.numpy as jnp
from jax import lax
from jax.experimental import pallas as pl
from jax.experimental.pallas import tpu as pltpu
from jax.sharding import PartitionSpec as P

HI = lax.Precision.HIGHEST
SUB = 8
LANES = 128
VMEM = pl.BlockSpec(memory_space=pltpu.VMEM)


def dot(a, b):
    return jnp.dot(a, b, precision=HI, preferred_element_type=jnp.float32)


def dot_t(a, b):
    dims = (((1,), (1,)), ((), ()))
    return lax.dot_general(a, b, dims, precision=HI, preferred_element_type=jnp.float32)


def factor_tile(blocks):
    shape = (SUB, LANES)
    lane = lax.broadcasted_iota(jnp.int32, shape, 1)
    sub = lax.broadcasted_iota(jnp.int32, shape, 0)
    count = len(blocks)
    blocks = list(blocks)
    upper, inverse = [], []
    for b in range(count):
        base = b * SUB
        here = blocks[b]
        across = [jnp.broadcast_to(here[:, base + k : base + k + 1], shape) for k in range(SUB)]
        rows = [jnp.broadcast_to(here[k : k + 1, :], shape) for k in range(SUB)]
        s = {}
        for k in range(SUB):
            for i in range(k, SUB):
                s[i, k] = jnp.broadcast_to(across[k][i : i + 1, :], shape)
        rinv, low, u, w = [], {}, [], []
        for k in range(SUB):
            rinv.append(lax.rsqrt(s[k, k]))
            for i in range(k + 1, SUB):
                low[i, k] = s[i, k] * rinv[k]
            for j in range(k + 1, SUB):
                for i in range(j, SUB):
                    s[i, j] = s[i, j] - low[i, k] * low[j, k]
            uk = rows[k]
            wk = jnp.where(lane < base, rows[k], jnp.where(lane == base + k, 1.0, 0.0))
            for m in range(k):
                uk = uk - low[k, m] * u[m]
                wk = wk - low[k, m] * w[m]
            u.append(uk * rinv[k])
            w.append(wk * rinv[k])
        u_block, w_block = u[0], w[0]
        for k in range(1, SUB):
            u_block = jnp.where(sub == k, u[k], u_block)
            w_block = jnp.where(sub == k, w[k], w_block)
        upper.append(jnp.where(lane >= sub + base, u_block, 0.0))
        inverse.append(w_block)
        if b + 1 == count:
            break
        q = [None] * SUB
        for k in reversed(range(SUB)):
            v = jnp.where(lane < base + SUB, w[k], u[k])
            for m in range(k + 1, SUB):
                v = v - low[m, k] * q[m]
            q[k] = v * rinv[k]
        keep = (lane < base) | (lane >= base + SUB)
        for i in range(b + 1, count):
            old = blocks[i]
            terms = [
                jnp.broadcast_to(old[:, base + k : base + k + 1], shape) * q[k] for k in range(SUB)
            ]
            while len(terms) > 1:
                terms = [terms[t] + terms[t + 1] for t in range(0, len(terms), 2)]
            blocks[i] = jnp.where(keep, old, 0.0) - terms[0]
    return upper, inverse


def eliminate(work, low_ref, inv_ref, diag_ref):
    size = work.shape[0]
    row_id = lax.broadcasted_iota(jnp.int32, (size, LANES), 0)
    col_id = lax.broadcasted_iota(jnp.int32, (LANES, size), 1)
    square = (LANES, LANES)
    on_diag = lax.broadcasted_iota(jnp.int32, square, 0) == lax.broadcasted_iota(
        jnp.int32, square, 1
    )

    def step(t, carry):
        base = pl.multiple_of(t * LANES, LANES)
        tile_rows = pl.ds(base, LANES)
        here = [work[pl.ds(base + SUB * i, SUB), tile_rows] for i in range(LANES // SUB)]
        up, inv = factor_tile(here)
        up = jnp.concatenate(up, axis=0)
        inv = jnp.concatenate(inv, axis=0)
        diag_ref[pl.ds(t, 1), :] = jnp.sum(jnp.where(on_diag, up, 0.0), axis=0, keepdims=True)
        across = dot(inv, work[tile_rows, :])
        below = dot_t(work[:, tile_rows], inv)
        below = jnp.where(row_id >= base + LANES, below, 0.0)
        low_ref[:, tile_rows] = below
        low_ref[tile_rows, tile_rows] = up.T
        inv_ref[tile_rows, :] = jnp.where(col_id < base, across, 0.0)
        inv_ref[tile_rows, tile_rows] = inv
        work[tile_rows, :] = across
        work[tile_rows, tile_rows] = inv
        across = work[tile_rows, :]
        work[:, tile_rows] = jnp.zeros((size, LANES), jnp.float32)
        work[...] = work[...] - dot(below, across)
        return carry

    lax.fori_loop(0, size // LANES, step, 0)


def first_kernel(d0_ref, low_ref, inv_ref, diag_ref, work):
    work[...] = d0_ref[...]
    eliminate(work, low_ref, inv_ref, diag_ref)


def second_kernel(d1_ref, inv0_ref, low_ref, inv_ref, diag_ref, work, low_here, inv_here):
    tile = inv0_ref.shape[0]
    inv0 = inv0_ref[...]
    left = dot_t(d1_ref[:, :tile], inv0)
    low_ref[:, :tile] = left
    work[...] = d1_ref[:, tile:] - dot_t(left, left)
    eliminate(work, low_here, inv_here, diag_ref)
    low_ref[:, tile:] = low_here[...]
    inv1 = inv_here[...]
    inv_ref[:, tile:] = inv1
    inv_ref[:, :tile] = -dot(inv1, dot(low_ref[:, :tile], inv0))


def call(kernel, name, outs, scratch, *args):
    flops = 4 * 256**3
    return pl.pallas_call(
        kernel,
        out_shape=[jax.ShapeDtypeStruct(shape, jnp.float32) for shape in outs],
        in_specs=[VMEM] * len(args),
        out_specs=[VMEM] * len(outs),
        scratch_shapes=[pltpu.VMEM(shape, jnp.float32) for shape in scratch],
        compiler_params=pltpu.CompilerParams(vmem_limit_bytes=32 * 1024 * 1024),
        cost_estimate=pl.CostEstimate(flops=flops, bytes_accessed=40 * 2**20, transcendentals=0),
        name=name,
    )(*args)


def send(value, hop, holders, extent):
    pairs = [(z, (z + hop) % extent) for z in holders]
    return lax.ppermute(value, "col", pairs), [target for _, target in pairs]


def spread_step(value, hops, holders, extent, position):
    arrived, targets = None, []
    for hop in hops:
        moved, reached = send(value, hop, holders, extent)
        arrived = moved if arrived is None else arrived + moved
        targets += reached
    is_new = jnp.zeros((), bool)
    for target in targets:
        is_new = is_new | (position == target)
    return jnp.where(is_new, arrived, value), sorted(set(holders) | set(targets))


def shards(covariance, observations):
    tile, wide = covariance.shape
    nrhs = observations.shape[0]
    rows = lax.axis_size("row")
    cols = lax.axis_size("col")
    row = lax.axis_index("row")
    col = lax.axis_index("col")
    part = tile // rows
    half = part // 2

    with jax.named_scope("scatter"):
        got = lax.all_to_all(
            covariance.reshape(rows, part, wide), "row", split_axis=0, concat_axis=0, tiled=True
        )
        first, second = got[0], got[1]
        obs_got = lax.all_to_all(
            observations.reshape(rows, half, -1), "row", split_axis=0, concat_axis=0, tiled=True
        )
        obs_piece = jnp.concatenate([obs_got[0], obs_got[1]], axis=0)

    with jax.named_scope("diag"):
        piece = jnp.concatenate([first[:, :tile], second], axis=1)
        holders = [0]
        piece, holders = spread_step(piece, (5, -5), holders, cols, col)
        piece, holders = spread_step(piece, (2, -2), holders, cols, col)
        piece, holders = spread_step(piece, (1,), [z for z in holders if (z + 1) % cols not in holders], cols, col)

    with jax.named_scope("columns"):
        col_piece = jnp.concatenate([first, second, obs_piece], axis=1)
        col_sent = jnp.broadcast_to(col_piece[None], (rows,) + col_piece.shape)
        col_all = lax.all_to_all(col_sent, "row", split_axis=0, concat_axis=0, tiled=True)
        col0 = col_all[:, :, :wide].reshape(tile, wide)
        col1 = col_all[:, :, wide : 2 * wide].reshape(tile, wide)
        obs0 = col_all[:, :half, 2 * wide :].reshape(nrhs, tile)
        obs1 = col_all[:, half:, 2 * wide :].reshape(nrhs, tile)

    with jax.named_scope("diag"):
        panel, piece = lax.optimization_barrier((covariance, piece))
        sent = jnp.broadcast_to(piece[None], (rows,) + piece.shape)
        whole = lax.all_to_all(sent, "row", split_axis=0, concat_axis=0, tiled=True)
        diag0 = whole[:, :, :tile].reshape(tile, tile)
        diag1 = whole[:, :, tile:].reshape(tile, wide)

    with jax.named_scope("rowpanel"):
        holders = [0]
        panel, holders = spread_step(panel, (5, -5), holders, cols, col)
        diag0, panel = lax.optimization_barrier((diag0, panel))
        panel, holders = spread_step(panel, (2, -2), holders, cols, col)

    low0, inv0, dg0 = call(
        first_kernel, "factor_first", [(tile, tile), (tile, tile), (tile // LANES, LANES)],
        [(tile, tile)], diag0,
    )
    inv0, panel = lax.optimization_barrier((inv0, panel))
    with jax.named_scope("rowpanel"):
        panel, _ = spread_step(panel, (1,), [z for z in holders if (z + 1) % cols not in holders], cols, col)
    low1, inv1, dg1 = call(
        second_kernel, "factor_second", [(tile, wide), (tile, wide), (tile // LANES, LANES)],
        [(tile, tile)] * 3, diag1, inv0,
    )

    low1, inv1, dg1, panel = lax.optimization_barrier((low1, inv1, dg1, panel))

    with jax.named_scope("solve"):
        y0 = dot(inv0, col0)
        y1 = dot(inv1[:, :tile], col0) + dot(inv1[:, tile:], col1)
        z0 = dot_t(obs0, inv0)
        z1 = dot_t(obs0, inv1[:, :tile]) + dot_t(obs1, inv1[:, tile:])
        x0 = dot_t(panel[:, :tile], inv0)
        x1 = dot_t(panel, inv1)

    with jax.named_scope("update"):
        trail = covariance - dot(x0, y0) - dot(x1, y1)
        first_rows = jnp.where(row == 0, jnp.pad(low0, ((0, 0), (0, tile))), low1)
        edge = jnp.where(row <= 1, first_rows, jnp.concatenate([x0, x1], axis=1))
        other = jnp.where(row <= 1, 0.0, trail)
        factored = jnp.where(col == 0, edge, other)
        reduced = observations - dot_t(z0, x0) - dot_t(z1, x1)
        solved = jnp.where(row == 0, z0, jnp.where(row == 1, z1, reduced))

    with jax.named_scope("terms"):
        logdet = 2.0 * (jnp.sum(jnp.log(dg0)) + jnp.sum(jnp.log(dg1)))
        quad = jnp.sum(z0 * z0, axis=1) + jnp.sum(z1 * z1, axis=1)
        site_terms = -(quad + logdet) / (4.0 * tile)
    return factored, solved, site_terms


def solution(mesh):
    in_specs = (P("row", "col"), P(None, "row"))
    out_specs = (P("row", "col"), P(None, "row"), P())
    return jax.shard_map(shards, mesh=mesh, in_specs=in_specs, out_specs=out_specs, check_vma=False)
```

```python
import jax
import jax.numpy as jnp
from jax import lax
from jax.experimental import pallas as pl
from jax.experimental.pallas import tpu as pltpu
from jax.sharding import PartitionSpec as P

HI = lax.Precision.HIGHEST
SUB = 8
LANES = 128
VMEM = pl.BlockSpec(memory_space=pltpu.VMEM)


def dot(a, b):
    return jnp.dot(a, b, precision=HI, preferred_element_type=jnp.float32)


def dot_t(a, b):
    dims = (((1,), (1,)), ((), ()))
    return lax.dot_general(a, b, dims, precision=HI, preferred_element_type=jnp.float32)


def factor_tile(blocks):
    shape = (SUB, LANES)
    lane = lax.broadcasted_iota(jnp.int32, shape, 1)
    sub = lax.broadcasted_iota(jnp.int32, shape, 0)
    count = len(blocks)
    blocks = list(blocks)
    upper, inverse = [], []
    for b in range(count):
        base = b * SUB
        here = blocks[b]
        across = [jnp.broadcast_to(here[:, base + k : base + k + 1], shape) for k in range(SUB)]
        rows = [jnp.broadcast_to(here[k : k + 1, :], shape) for k in range(SUB)]
        s = {}
        for k in range(SUB):
            for i in range(k, SUB):
                s[i, k] = jnp.broadcast_to(across[k][i : i + 1, :], shape)
        rinv, low, u, w = [], {}, [], []
        for k in range(SUB):
            rinv.append(lax.rsqrt(s[k, k]))
            for i in range(k + 1, SUB):
                low[i, k] = s[i, k] * rinv[k]
            for j in range(k + 1, SUB):
                for i in range(j, SUB):
                    s[i, j] = s[i, j] - low[i, k] * low[j, k]
            uk = rows[k]
            wk = jnp.where(lane < base, rows[k], jnp.where(lane == base + k, 1.0, 0.0))
            for m in range(k):
                uk = uk - low[k, m] * u[m]
                wk = wk - low[k, m] * w[m]
            u.append(uk * rinv[k])
            w.append(wk * rinv[k])
        u_block, w_block = u[0], w[0]
        for k in range(1, SUB):
            u_block = jnp.where(sub == k, u[k], u_block)
            w_block = jnp.where(sub == k, w[k], w_block)
        upper.append(jnp.where(lane >= sub + base, u_block, 0.0))
        inverse.append(w_block)
        if b + 1 == count:
            break
        q = [None] * SUB
        for k in reversed(range(SUB)):
            v = jnp.where(lane < base + SUB, w[k], u[k])
            for m in range(k + 1, SUB):
                v = v - low[m, k] * q[m]
            q[k] = v * rinv[k]
        keep = (lane < base) | (lane >= base + SUB)
        for i in range(b + 1, count):
            old = blocks[i]
            terms = [
                jnp.broadcast_to(old[:, base + k : base + k + 1], shape) * q[k] for k in range(SUB)
            ]
            while len(terms) > 1:
                terms = [terms[t] + terms[t + 1] for t in range(0, len(terms), 2)]
            blocks[i] = jnp.where(keep, old, 0.0) - terms[0]
    return upper, inverse


def eliminate(work, low_ref, inv_ref, diag_ref):
    size = work.shape[0]
    row_id = lax.broadcasted_iota(jnp.int32, (size, LANES), 0)
    col_id = lax.broadcasted_iota(jnp.int32, (LANES, size), 1)
    square = (LANES, LANES)
    on_diag = lax.broadcasted_iota(jnp.int32, square, 0) == lax.broadcasted_iota(
        jnp.int32, square, 1
    )

    def step(t, carry):
        base = pl.multiple_of(t * LANES, LANES)
        tile_rows = pl.ds(base, LANES)
        here = [work[pl.ds(base + SUB * i, SUB), tile_rows] for i in range(LANES // SUB)]
        up, inv = factor_tile(here)
        up = jnp.concatenate(up, axis=0)
        inv = jnp.concatenate(inv, axis=0)
        diag_ref[pl.ds(t, 1), :] = jnp.sum(jnp.where(on_diag, up, 0.0), axis=0, keepdims=True)
        across = dot(inv, work[tile_rows, :])
        below = dot_t(work[:, tile_rows], inv)
        below = jnp.where(row_id >= base + LANES, below, 0.0)
        low_ref[:, tile_rows] = below
        low_ref[tile_rows, tile_rows] = up.T
        inv_ref[tile_rows, :] = jnp.where(col_id < base, across, 0.0)
        inv_ref[tile_rows, tile_rows] = inv
        work[tile_rows, :] = across
        work[tile_rows, tile_rows] = inv
        across = work[tile_rows, :]
        work[:, tile_rows] = jnp.zeros((size, LANES), jnp.float32)
        work[...] = work[...] - dot(below, across)
        return carry

    lax.fori_loop(0, size // LANES, step, 0)


def first_kernel(d_ref, low_ref, inv_ref, diag_ref, work):
    tile = work.shape[0]
    work[...] = d_ref[:, :tile]
    eliminate(work, low_ref, inv_ref, diag_ref)


def second_kernel(d_ref, inv0_ref, low_ref, inv_ref, diag_ref, work, low_here, inv_here):
    tile = inv0_ref.shape[0]
    inv0 = inv0_ref[...]
    left = dot_t(d_ref[:, tile : 2 * tile], inv0)
    low_ref[:, :tile] = left
    work[...] = d_ref[:, 2 * tile : 3 * tile] - dot_t(left, left)
    eliminate(work, low_here, inv_here, diag_ref)
    low_ref[:, tile:] = low_here[...]
    inv1 = inv_here[...]
    inv_ref[:, tile:] = inv1
    inv_ref[:, :tile] = -dot(inv1, dot(low_ref[:, :tile], inv0))


def finish_kernel(
    ids_ref, panel_ref, moved_ref, wide_ref, low0_ref, inv0_ref, diag0_ref, low1_ref, inv1_ref,
    diag1_ref, cov_ref, obs_ref, out_ref, solved_ref, site_ref, rows_here,
):
    tile, wide = cov_ref.shape
    nrhs = obs_ref.shape[0]
    row, col, is_new = ids_ref[0], ids_ref[1], ids_ref[2]
    inv0 = inv0_ref[...]
    inv10 = inv1_ref[:, :tile]
    inv11 = inv1_ref[:, tile:]

    rows_here[...] = panel_ref[...]

    @pl.when(is_new == 1)
    def _():
        rows_here[...] = moved_ref[...]

    obs_both = wide_ref[:, 2 * wide : 2 * wide + 2 * nrhs]
    z0 = dot(inv0, obs_both)[:, :nrhs]
    z1 = dot(inv10, obs_both)[:, :nrhs] + dot(inv11, obs_both)[:, nrhs:]
    quad = jnp.sum(z0 * z0 + z1 * z1, axis=0, keepdims=True)
    logs = jnp.log(diag0_ref[...]) + jnp.log(diag1_ref[...])
    site_ref[...] = -(quad + 2.0 * jnp.sum(logs)) / (4.0 * tile)

    @pl.when(row == 0)
    def _():
        solved_ref[...] = z0.T

    @pl.when(row == 1)
    def _():
        solved_ref[...] = z1.T

    @pl.when(row <= 1)
    def _():
        out_ref[...] = jnp.zeros((tile, wide), jnp.float32)

    @pl.when((row == 0) & (col == 0))
    def _():
        out_ref[:, :tile] = low0_ref[...]

    @pl.when((row == 1) & (col == 0))
    def _():
        out_ref[...] = low1_ref[...]

    @pl.when(row > 1)
    def _():
        x0 = dot_t(rows_here[:, :tile], inv0)
        x1 = dot_t(rows_here[...], inv1_ref[...])
        solved_ref[...] = obs_ref[...] - (dot(x0, z0) + dot(x1, z1)).T

        @pl.when(col == 0)
        def _():
            out_ref[:, :tile] = x0
            out_ref[:, tile:] = x1

        @pl.when(col > 0)
        def _():
            c0 = wide_ref[:, :wide]
            y0 = dot(inv0, c0)
            y1 = dot(inv10, c0) + dot(inv11, wide_ref[:, wide : 2 * wide])
            out_ref[...] = cov_ref[...] - dot(x0, y0) - dot(x1, y1)


def call(kernel, name, outs, scratch, *args, ids=None):
    flops = 4 * 256**3
    specs = [VMEM] * len(args)
    if ids is not None:
        specs = [pl.BlockSpec(memory_space=pltpu.SMEM)] + specs
        args = (ids,) + args
    return pl.pallas_call(
        kernel,
        out_shape=[jax.ShapeDtypeStruct(shape, jnp.float32) for shape in outs],
        in_specs=specs,
        out_specs=[VMEM] * len(outs),
        scratch_shapes=[pltpu.VMEM(shape, jnp.float32) for shape in scratch],
        compiler_params=pltpu.CompilerParams(vmem_limit_bytes=40 * 1024 * 1024),
        cost_estimate=pl.CostEstimate(flops=flops, bytes_accessed=40 * 2**20, transcendentals=0),
        name=name,
    )(*args)


def send(value, hop, holders, extent):
    pairs = [(z, (z + hop) % extent) for z in holders]
    return lax.ppermute(value, "col", pairs), [target for _, target in pairs]


def spread_step(value, hops, holders, extent, position):
    arrived, targets = None, []
    for hop in hops:
        moved, reached = send(value, hop, holders, extent)
        arrived = moved if arrived is None else arrived + moved
        targets += reached
    is_new = jnp.zeros((), bool)
    for target in targets:
        is_new = is_new | (position == target)
    return jnp.where(is_new, arrived, value), sorted(set(holders) | set(targets))


def shards(covariance, observations):
    tile, wide = covariance.shape
    nrhs = observations.shape[0]
    rows = lax.axis_size("row")
    cols = lax.axis_size("col")
    row = lax.axis_index("row")
    col = lax.axis_index("col")
    part = tile // rows

    def exchange(value):
        return lax.all_to_all(value, "row", split_axis=0, concat_axis=0, tiled=True)

    with jax.named_scope("scatter"):
        got = exchange(covariance.reshape(rows, part, wide))
        first, second = got[0], got[1]
        obs_parts = jnp.pad(observations.T, ((0, 0), (0, LANES - nrhs))).reshape(rows, part, LANES)

    with jax.named_scope("diag"):
        piece = jnp.concatenate([first[:, :tile], second], axis=1)
        holders = [0]
        piece, holders = spread_step(piece, (5, -5), holders, cols, col)
        piece, holders = spread_step(piece, (2, -2), holders, cols, col)
        last = [z for z in holders if (z + 1) % cols not in holders]
        piece, _ = spread_step(piece, (1,), last, cols, col)
        panel, piece = lax.optimization_barrier((covariance, piece))
        sent = jnp.broadcast_to(piece[None], (rows,) + piece.shape)
        whole = exchange(jnp.concatenate([sent, obs_parts], axis=2))
        diag = whole.reshape(tile, -1)

    with jax.named_scope("columns"):
        start = 3 * tile
        col_piece = jnp.concatenate(
            [first, second, whole[0, :, start : start + nrhs], whole[1, :, start : start + nrhs]],
            axis=1,
        )
        columns = exchange(jnp.broadcast_to(col_piece[None], (rows,) + col_piece.shape))
        columns = columns.reshape(tile, -1)

    with jax.named_scope("rowpanel"):
        panel, holders = spread_step(panel, (5, -5), [0], cols, col)
        diag, panel = lax.optimization_barrier((diag, panel))
        panel, holders = spread_step(panel, (2, -2), holders, cols, col)

    low0, inv0, diag0 = call(
        first_kernel, "factor_first", [(tile, tile), (tile, tile), (tile // LANES, LANES)],
        [(tile, tile)], diag,
    )
    inv0, panel = lax.optimization_barrier((inv0, panel))
    with jax.named_scope("rowpanel"):
        moved, reached = send(panel, 1, last, cols)
    low1, inv1, diag1 = call(
        second_kernel, "factor_second", [(tile, wide), (tile, wide), (tile // LANES, LANES)],
        [(tile, tile)] * 3, diag, inv0,
    )

    is_new = jnp.zeros((), bool)
    for target in reached:
        is_new = is_new | (col == target)
    ids = jnp.stack([row, col, is_new.astype(jnp.int32)])
    factored, solved, site = call(
        finish_kernel, "finish", [(tile, wide), (nrhs, tile), (1, nrhs)], [(tile, wide)],
        panel, moved, columns, low0, inv0, diag0, low1, inv1, diag1, covariance, observations,
        ids=ids,
    )
    return factored, solved, site.reshape(nrhs)


def solution(mesh):
    in_specs = (P("row", "col"), P(None, "row"))
    out_specs = (P("row", "col"), P(None, "row"), P())
    return jax.shard_map(shards, mesh=mesh, in_specs=in_specs, out_specs=out_specs, check_vma=False)
```

```python
import jax
import jax.numpy as jnp
from jax import lax
from jax.experimental import pallas as pl
from jax.experimental.pallas import tpu as pltpu
from jax.sharding import PartitionSpec as P

HI = lax.Precision.HIGHEST
SUB = 8
LANES = 128
VMEM = pl.BlockSpec(memory_space=pltpu.VMEM)


def dot(a, b):
    return jnp.dot(a, b, precision=HI, preferred_element_type=jnp.float32)


def dot_t(a, b):
    dims = (((1,), (1,)), ((), ()))
    return lax.dot_general(a, b, dims, precision=HI, preferred_element_type=jnp.float32)


def factor_tile(blocks):
    shape = (SUB, LANES)
    lane = lax.broadcasted_iota(jnp.int32, shape, 1)
    sub = lax.broadcasted_iota(jnp.int32, shape, 0)
    count = len(blocks)
    blocks = list(blocks)
    upper, inverse = [], []
    for b in range(count):
        base = b * SUB
        here = blocks[b]
        across = [jnp.broadcast_to(here[:, base + k : base + k + 1], shape) for k in range(SUB)]
        rows = [jnp.broadcast_to(here[k : k + 1, :], shape) for k in range(SUB)]
        s = {}
        for k in range(SUB):
            for i in range(k, SUB):
                s[i, k] = jnp.broadcast_to(across[k][i : i + 1, :], shape)
        rinv, low, u, w = [], {}, [], []
        for k in range(SUB):
            rinv.append(lax.rsqrt(s[k, k]))
            for i in range(k + 1, SUB):
                low[i, k] = s[i, k] * rinv[k]
            for j in range(k + 1, SUB):
                for i in range(j, SUB):
                    s[i, j] = s[i, j] - low[i, k] * low[j, k]
            uk = rows[k]
            wk = jnp.where(lane < base, rows[k], jnp.where(lane == base + k, 1.0, 0.0))
            for m in range(k):
                uk = uk - low[k, m] * u[m]
                wk = wk - low[k, m] * w[m]
            u.append(uk * rinv[k])
            w.append(wk * rinv[k])
        u_block, w_block = u[0], w[0]
        for k in range(1, SUB):
            u_block = jnp.where(sub == k, u[k], u_block)
            w_block = jnp.where(sub == k, w[k], w_block)
        upper.append(jnp.where(lane >= sub + base, u_block, 0.0))
        inverse.append(w_block)
        if b + 1 == count:
            break
        q = [None] * SUB
        for k in reversed(range(SUB)):
            v = jnp.where(lane < base + SUB, w[k], u[k])
            for m in range(k + 1, SUB):
                v = v - low[m, k] * q[m]
            q[k] = v * rinv[k]
        keep = (lane < base) | (lane >= base + SUB)
        for i in range(b + 1, count):
            old = blocks[i]
            terms = [
                jnp.broadcast_to(old[:, base + k : base + k + 1], shape) * q[k] for k in range(SUB)
            ]
            while len(terms) > 1:
                terms = [terms[t] + terms[t + 1] for t in range(0, len(terms), 2)]
            blocks[i] = jnp.where(keep, old, 0.0) - terms[0]
    return upper, inverse


def eliminate(work, low_ref, inv_ref, diag_ref):
    size = work.shape[0]
    row_id = lax.broadcasted_iota(jnp.int32, (size, LANES), 0)
    col_id = lax.broadcasted_iota(jnp.int32, (LANES, size), 1)
    square = (LANES, LANES)
    on_diag = lax.broadcasted_iota(jnp.int32, square, 0) == lax.broadcasted_iota(
        jnp.int32, square, 1
    )

    def step(t, carry):
        base = pl.multiple_of(t * LANES, LANES)
        tile_rows = pl.ds(base, LANES)
        here = [work[pl.ds(base + SUB * i, SUB), tile_rows] for i in range(LANES // SUB)]
        up, inv = factor_tile(here)
        up = jnp.concatenate(up, axis=0)
        inv = jnp.concatenate(inv, axis=0)
        diag_ref[pl.ds(t, 1), :] = jnp.sum(jnp.where(on_diag, up, 0.0), axis=0, keepdims=True)
        across = dot(inv, work[tile_rows, :])
        below = dot_t(work[:, tile_rows], inv)
        below = jnp.where(row_id >= base + LANES, below, 0.0)
        low_ref[:, tile_rows] = below
        low_ref[tile_rows, tile_rows] = up.T
        inv_ref[tile_rows, :] = jnp.where(col_id < base, across, 0.0)
        inv_ref[tile_rows, tile_rows] = inv
        work[tile_rows, :] = across
        work[tile_rows, tile_rows] = inv
        across = work[tile_rows, :]
        work[:, tile_rows] = jnp.zeros((size, LANES), jnp.float32)
        work[...] = work[...] - dot(below, across)
        return carry

    lax.fori_loop(0, size // LANES, step, 0)


def first_kernel(d_ref, low_ref, inv_ref, diag_ref, work):
    tile = work.shape[0]
    work[...] = d_ref[:, :tile]
    eliminate(work, low_ref, inv_ref, diag_ref)


def second_kernel(d_ref, inv0_ref, low_ref, inv_ref, diag_ref, work, low_here, inv_here):
    tile = inv0_ref.shape[0]
    inv0 = inv0_ref[...]
    left = dot_t(d_ref[:, tile : 2 * tile], inv0)
    low_ref[:, :tile] = left
    work[...] = d_ref[:, 2 * tile : 3 * tile] - dot_t(left, left)
    eliminate(work, low_here, inv_here, diag_ref)
    low_ref[:, tile:] = low_here[...]
    inv1 = inv_here[...]
    inv_ref[:, tile:] = inv1
    inv_ref[:, :tile] = -dot(inv1, dot(low_ref[:, :tile], inv0))


def finish_kernel(
    ids_ref, panel_ref, moved_ref, wide_ref, low0_ref, inv0_ref, diag0_ref, low1_ref, inv1_ref,
    diag1_ref, cov_ref, obs_ref, out_ref, solved_ref, site_ref, rows_here,
):
    tile, wide = cov_ref.shape
    nrhs = obs_ref.shape[0]
    row, col, is_new = ids_ref[0], ids_ref[1], ids_ref[2]
    inv0 = inv0_ref[...]
    inv10 = inv1_ref[:, :tile]
    inv11 = inv1_ref[:, tile:]

    rows_here[...] = panel_ref[...]

    @pl.when(is_new == 1)
    def _():
        rows_here[...] = moved_ref[...]

    obs_both = wide_ref[:, 2 * wide : 2 * wide + 2 * nrhs]
    z0 = dot(inv0, obs_both)[:, :nrhs]
    z1 = dot(inv10, obs_both)[:, :nrhs] + dot(inv11, obs_both)[:, nrhs:]
    quad = jnp.sum(z0 * z0 + z1 * z1, axis=0, keepdims=True)
    logs = jnp.log(diag0_ref[...]) + jnp.log(diag1_ref[...])
    site_ref[...] = -(quad + 2.0 * jnp.sum(logs)) / (4.0 * tile)

    @pl.when(row == 0)
    def _():
        solved_ref[...] = z0.T

    @pl.when(row == 1)
    def _():
        solved_ref[...] = z1.T

    @pl.when(row <= 1)
    def _():
        out_ref[...] = jnp.zeros((tile, wide), jnp.float32)

    @pl.when((row == 0) & (col == 0))
    def _():
        out_ref[:, :tile] = low0_ref[...]

    @pl.when((row == 1) & (col == 0))
    def _():
        out_ref[...] = low1_ref[...]

    @pl.when(row > 1)
    def _():
        x0 = dot_t(rows_here[:, :tile], inv0)
        x1 = dot_t(rows_here[...], inv1_ref[...])
        solved_ref[...] = obs_ref[...] - (dot(x0, z0) + dot(x1, z1)).T

        @pl.when(col == 0)
        def _():
            out_ref[:, :tile] = x0
            out_ref[:, tile:] = x1

        @pl.when(col > 0)
        def _():
            c0 = wide_ref[:, :wide]
            y0 = dot(inv0, c0)
            y1 = dot(inv10, c0) + dot(inv11, wide_ref[:, wide : 2 * wide])
            out_ref[...] = cov_ref[...] - dot(x0, y0) - dot(x1, y1)


def call(kernel, name, outs, scratch, *args, ids=None):
    flops = 4 * 256**3
    specs = [VMEM] * len(args)
    if ids is not None:
        specs = [pl.BlockSpec(memory_space=pltpu.SMEM)] + specs
        args = (ids,) + args
    return pl.pallas_call(
        kernel,
        out_shape=[jax.ShapeDtypeStruct(shape, jnp.float32) for shape in outs],
        in_specs=specs,
        out_specs=[VMEM] * len(outs),
        scratch_shapes=[pltpu.VMEM(shape, jnp.float32) for shape in scratch],
        compiler_params=pltpu.CompilerParams(vmem_limit_bytes=16 * 1024 * 1024),
        cost_estimate=pl.CostEstimate(flops=flops, bytes_accessed=40 * 2**20, transcendentals=0),
        name=name,
    )(*args)


def send(value, hop, holders, extent):
    pairs = [(z, (z + hop) % extent) for z in holders]
    return lax.ppermute(value, "col", pairs), [target for _, target in pairs]


def spread_step(value, hops, holders, extent, position):
    arrived, targets = None, []
    for hop in hops:
        moved, reached = send(value, hop, holders, extent)
        arrived = moved if arrived is None else arrived + moved
        targets += reached
    is_new = jnp.zeros((), bool)
    for target in targets:
        is_new = is_new | (position == target)
    return jnp.where(is_new, arrived, value), sorted(set(holders) | set(targets))


def shards(covariance, observations):
    tile, wide = covariance.shape
    nrhs = observations.shape[0]
    rows = lax.axis_size("row")
    cols = lax.axis_size("col")
    row = lax.axis_index("row")
    col = lax.axis_index("col")
    part = tile // rows

    def exchange(value):
        return lax.all_to_all(value, "row", split_axis=0, concat_axis=0, tiled=True)

    with jax.named_scope("scatter"):
        got = exchange(covariance.reshape(rows, part, wide))
        first, second = got[0], got[1]
        obs_parts = jnp.pad(observations.T, ((0, 0), (0, LANES - nrhs))).reshape(rows, part, LANES)

    with jax.named_scope("diag"):
        piece = jnp.concatenate([first[:, :tile], second], axis=1)
        holders = [0]
        piece, holders = spread_step(piece, (5, -5), holders, cols, col)
        piece, holders = spread_step(piece, (2, -2), holders, cols, col)
        last = [z for z in holders if (z + 1) % cols not in holders]
        piece, _ = spread_step(piece, (1,), last, cols, col)
        panel, piece = lax.optimization_barrier((covariance, piece))
        sent = jnp.broadcast_to(piece[None], (rows,) + piece.shape)
        whole = exchange(jnp.concatenate([sent, obs_parts], axis=2))
        diag = whole.reshape(tile, -1)

    with jax.named_scope("columns"):
        start = 3 * tile
        col_piece = jnp.concatenate(
            [first, second, whole[0, :, start : start + nrhs], whole[1, :, start : start + nrhs]],
            axis=1,
        )
        columns = exchange(jnp.broadcast_to(col_piece[None], (rows,) + col_piece.shape))
        columns = columns.reshape(tile, -1)

    with jax.named_scope("rowpanel"):
        panel, holders = spread_step(panel, (5, -5), [0], cols, col)
        panel, holders = spread_step(panel, (2, -2), holders, cols, col)

    low0, inv0, diag0 = call(
        first_kernel, "factor_first", [(tile, tile), (tile, tile), (tile // LANES, LANES)],
        [(tile, tile)], diag,
    )
    inv0, panel, columns = lax.optimization_barrier((inv0, panel, columns))
    with jax.named_scope("rowpanel"):
        moved, reached = send(panel, 1, last, cols)
    low1, inv1, diag1 = call(
        second_kernel, "factor_second", [(tile, wide), (tile, wide), (tile // LANES, LANES)],
        [(tile, tile)] * 3, diag, inv0,
    )

    is_new = jnp.zeros((), bool)
    for target in reached:
        is_new = is_new | (col == target)
    ids = jnp.stack([row, col, is_new.astype(jnp.int32)])
    factored, solved, site = call(
        finish_kernel, "finish", [(tile, wide), (nrhs, tile), (1, nrhs)], [(tile, wide)],
        panel, moved, columns, low0, inv0, diag0, low1, inv1, diag1, covariance, observations,
        ids=ids,
    )
    return factored, solved, site.reshape(nrhs)


def solution(mesh):
    in_specs = (P("row", "col"), P(None, "row"))
    out_specs = (P("row", "col"), P(None, "row"), P())
    return jax.shard_map(shards, mesh=mesh, in_specs=in_specs, out_specs=out_specs, check_vma=False)
```

```python
import jax
import jax.numpy as jnp
from jax import lax
from jax.experimental import pallas as pl
from jax.experimental.pallas import tpu as pltpu
from jax.sharding import PartitionSpec as P

HI = lax.Precision.HIGHEST
SUB = 8
GROUP = 4
LANES = 128
VMEM = pl.BlockSpec(memory_space=pltpu.VMEM)


def dot(a, b):
    return jnp.dot(a, b, precision=HI, preferred_element_type=jnp.float32)


def dot_t(a, b):
    dims = (((1,), (1,)), ((), ()))
    return lax.dot_general(a, b, dims, precision=HI, preferred_element_type=jnp.float32)


def factor_tile(blocks):
    shape = (SUB, LANES)
    lane = lax.broadcasted_iota(jnp.int32, shape, 1)
    sub = lax.broadcasted_iota(jnp.int32, shape, 0)
    count = len(blocks)
    blocks = list(blocks)
    upper, inverse, left, right = [], [], [], []
    for b in range(count):
        base = b * SUB
        start = b // GROUP * GROUP
        stop = start + GROUP
        here = blocks[b]
        across = [jnp.broadcast_to(here[:, base + k : base + k + 1], shape) for k in range(SUB)]
        rows = [jnp.broadcast_to(here[k : k + 1, :], shape) for k in range(SUB)]
        s = {}
        for k in range(SUB):
            for i in range(k, SUB):
                s[i, k] = jnp.broadcast_to(across[k][i : i + 1, :], shape)
        rinv, low, u, w = [], {}, [], []
        for k in range(SUB):
            rinv.append(lax.rsqrt(s[k, k]))
            for i in range(k + 1, SUB):
                low[i, k] = s[i, k] * rinv[k]
            for j in range(k + 1, SUB):
                for i in range(j, SUB):
                    s[i, j] = s[i, j] - low[i, k] * low[j, k]
            uk = rows[k]
            wk = jnp.where(lane < base, rows[k], jnp.where(lane == base + k, 1.0, 0.0))
            for m in range(k):
                uk = uk - low[k, m] * u[m]
                wk = wk - low[k, m] * w[m]
            u.append(uk * rinv[k])
            w.append(wk * rinv[k])
        u_block, w_block = u[0], w[0]
        for k in range(1, SUB):
            u_block = jnp.where(sub == k, u[k], u_block)
            w_block = jnp.where(sub == k, w[k], w_block)
        upper.append(jnp.where(lane >= sub + base, u_block, 0.0))
        inverse.append(w_block)
        left.append(u_block)
        right.append(jnp.where(lane < stop * SUB, w_block, u_block))
        if b + 1 == stop:
            if stop < count:
                far = lax.dot_general(
                    jnp.concatenate(left[start:], axis=0), jnp.concatenate(right[start:], axis=0),
                    (((0,), (0,)), ((), ())), precision=HI, preferred_element_type=jnp.float32,
                )
                keep = (lane < start * SUB) | (lane >= stop * SUB)
                for i in range(stop, count):
                    blocks[i] = jnp.where(keep, blocks[i], 0.0) - far[i * SUB : (i + 1) * SUB]
            continue
        q = [None] * SUB
        for k in reversed(range(SUB)):
            v = jnp.where(lane < base + SUB, w[k], u[k])
            for m in range(k + 1, SUB):
                v = v - low[m, k] * q[m]
            q[k] = v * rinv[k]
        keep = (lane < base) | (lane >= base + SUB)
        for i in range(b + 1, stop):
            old = blocks[i]
            terms = [
                jnp.broadcast_to(old[:, base + k : base + k + 1], shape) * q[k] for k in range(SUB)
            ]
            while len(terms) > 1:
                terms = [terms[t] + terms[t + 1] for t in range(0, len(terms), 2)]
            blocks[i] = jnp.where(keep, old, 0.0) - terms[0]
    return upper, inverse


def eliminate(work, low_ref, inv_ref, diag_ref):
    size = work.shape[0]
    row_id = lax.broadcasted_iota(jnp.int32, (size, LANES), 0)
    col_id = lax.broadcasted_iota(jnp.int32, (LANES, size), 1)
    square = (LANES, LANES)
    on_diag = lax.broadcasted_iota(jnp.int32, square, 0) == lax.broadcasted_iota(
        jnp.int32, square, 1
    )

    def step(t, carry):
        base = pl.multiple_of(t * LANES, LANES)
        tile_rows = pl.ds(base, LANES)
        here = [work[pl.ds(base + SUB * i, SUB), tile_rows] for i in range(LANES // SUB)]
        up, inv = factor_tile(here)
        up = jnp.concatenate(up, axis=0)
        inv = jnp.concatenate(inv, axis=0)
        diag_ref[pl.ds(t, 1), :] = jnp.sum(jnp.where(on_diag, up, 0.0), axis=0, keepdims=True)
        across = dot(inv, work[tile_rows, :])
        below = dot_t(work[:, tile_rows], inv)
        below = jnp.where(row_id >= base + LANES, below, 0.0)
        low_ref[:, tile_rows] = below
        low_ref[tile_rows, tile_rows] = up.T
        inv_ref[tile_rows, :] = jnp.where(col_id < base, across, 0.0)
        inv_ref[tile_rows, tile_rows] = inv
        work[tile_rows, :] = across
        work[tile_rows, tile_rows] = inv
        across = work[tile_rows, :]
        work[:, tile_rows] = jnp.zeros((size, LANES), jnp.float32)
        work[...] = work[...] - dot(below, across)
        return carry

    lax.fori_loop(0, size // LANES, step, 0)


def first_kernel(d_ref, low_ref, inv_ref, diag_ref, work):
    tile = work.shape[0]
    work[...] = d_ref[:, :tile]
    eliminate(work, low_ref, inv_ref, diag_ref)


def second_kernel(d_ref, inv0_ref, low_ref, inv_ref, diag_ref, work, low_here, inv_here):
    tile = inv0_ref.shape[0]
    inv0 = inv0_ref[...]
    left = dot_t(d_ref[:, tile : 2 * tile], inv0)
    low_ref[:, :tile] = left
    work[...] = d_ref[:, 2 * tile : 3 * tile] - dot_t(left, left)
    eliminate(work, low_here, inv_here, diag_ref)
    low_ref[:, tile:] = low_here[...]
    inv1 = inv_here[...]
    inv_ref[:, tile:] = inv1
    inv_ref[:, :tile] = -dot(inv1, dot(low_ref[:, :tile], inv0))


def finish_kernel(
    ids_ref, panel_ref, moved_ref, wide_ref, low0_ref, inv0_ref, diag0_ref, low1_ref, inv1_ref,
    diag1_ref, cov_ref, obs_ref, out_ref, solved_ref, site_ref, rows_here,
):
    tile, wide = cov_ref.shape
    nrhs = obs_ref.shape[0]
    row, col, is_new = ids_ref[0], ids_ref[1], ids_ref[2]
    inv0 = inv0_ref[...]
    inv10 = inv1_ref[:, :tile]
    inv11 = inv1_ref[:, tile:]

    rows_here[...] = panel_ref[...]

    @pl.when(is_new == 1)
    def _():
        rows_here[...] = moved_ref[...]

    obs_both = wide_ref[:, 2 * wide : 2 * wide + 2 * nrhs]
    z0 = dot(inv0, obs_both)[:, :nrhs]
    z1 = dot(inv10, obs_both)[:, :nrhs] + dot(inv11, obs_both)[:, nrhs:]
    quad = jnp.sum(z0 * z0 + z1 * z1, axis=0, keepdims=True)
    logs = jnp.log(diag0_ref[...]) + jnp.log(diag1_ref[...])
    site_ref[...] = -(quad + 2.0 * jnp.sum(logs)) / (4.0 * tile)

    @pl.when(row == 0)
    def _():
        solved_ref[...] = z0.T

    @pl.when(row == 1)
    def _():
        solved_ref[...] = z1.T

    @pl.when(row <= 1)
    def _():
        out_ref[...] = jnp.zeros((tile, wide), jnp.float32)

    @pl.when((row == 0) & (col == 0))
    def _():
        out_ref[:, :tile] = low0_ref[...]

    @pl.when((row == 1) & (col == 0))
    def _():
        out_ref[...] = low1_ref[...]

    @pl.when(row > 1)
    def _():
        x0 = dot_t(rows_here[:, :tile], inv0)
        x1 = dot_t(rows_here[...], inv1_ref[...])
        solved_ref[...] = obs_ref[...] - (dot(x0, z0) + dot(x1, z1)).T

        @pl.when(col == 0)
        def _():
            out_ref[:, :tile] = x0
            out_ref[:, tile:] = x1

        @pl.when(col > 0)
        def _():
            c0 = wide_ref[:, :wide]
            y0 = dot(inv0, c0)
            y1 = dot(inv10, c0) + dot(inv11, wide_ref[:, wide : 2 * wide])
            out_ref[...] = cov_ref[...] - dot(x0, y0) - dot(x1, y1)


def call(kernel, name, outs, scratch, *args, ids=None):
    flops = 4 * 256**3
    specs = [VMEM] * len(args)
    if ids is not None:
        specs = [pl.BlockSpec(memory_space=pltpu.SMEM)] + specs
        args = (ids,) + args
    return pl.pallas_call(
        kernel,
        out_shape=[jax.ShapeDtypeStruct(shape, jnp.float32) for shape in outs],
        in_specs=specs,
        out_specs=[VMEM] * len(outs),
        scratch_shapes=[pltpu.VMEM(shape, jnp.float32) for shape in scratch],
        compiler_params=pltpu.CompilerParams(vmem_limit_bytes=16 * 1024 * 1024),
        cost_estimate=pl.CostEstimate(flops=flops, bytes_accessed=40 * 2**20, transcendentals=0),
        name=name,
    )(*args)


def send(value, hop, holders, extent):
    pairs = [(z, (z + hop) % extent) for z in holders]
    return lax.ppermute(value, "col", pairs), [target for _, target in pairs]


def spread_step(value, hops, holders, extent, position):
    arrived, targets = None, []
    for hop in hops:
        moved, reached = send(value, hop, holders, extent)
        arrived = moved if arrived is None else arrived + moved
        targets += reached
    is_new = jnp.zeros((), bool)
    for target in targets:
        is_new = is_new | (position == target)
    return jnp.where(is_new, arrived, value), sorted(set(holders) | set(targets))


def shards(covariance, observations):
    tile, wide = covariance.shape
    nrhs = observations.shape[0]
    rows = lax.axis_size("row")
    cols = lax.axis_size("col")
    row = lax.axis_index("row")
    col = lax.axis_index("col")
    part = tile // rows

    def exchange(value):
        return lax.all_to_all(value, "row", split_axis=0, concat_axis=0, tiled=True)

    with jax.named_scope("scatter"):
        got = exchange(covariance.reshape(rows, part, wide))
        first, second = got[0], got[1]
        obs_parts = jnp.pad(observations.T, ((0, 0), (0, LANES - nrhs))).reshape(rows, part, LANES)

    with jax.named_scope("diag"):
        piece = jnp.concatenate([first[:, :tile], second], axis=1)
        holders = [0]
        piece, holders = spread_step(piece, (5, -5), holders, cols, col)
        piece, holders = spread_step(piece, (2, -2), holders, cols, col)
        last = [z for z in holders if (z + 1) % cols not in holders]
        piece, _ = spread_step(piece, (1,), last, cols, col)
        panel, piece = lax.optimization_barrier((covariance, piece))
        sent = jnp.broadcast_to(piece[None], (rows,) + piece.shape)
        whole = exchange(jnp.concatenate([sent, obs_parts], axis=2))
        diag = whole.reshape(tile, -1)

    with jax.named_scope("columns"):
        start = 3 * tile
        col_piece = jnp.concatenate(
            [first, second, whole[0, :, start : start + nrhs], whole[1, :, start : start + nrhs]],
            axis=1,
        )
        columns = exchange(jnp.broadcast_to(col_piece[None], (rows,) + col_piece.shape))
        columns = columns.reshape(tile, -1)

    with jax.named_scope("rowpanel"):
        panel, holders = spread_step(panel, (5, -5), [0], cols, col)
        panel, holders = spread_step(panel, (2, -2), holders, cols, col)

    low0, inv0, diag0 = call(
        first_kernel, "factor_first", [(tile, tile), (tile, tile), (tile // LANES, LANES)],
        [(tile, tile)], diag,
    )
    inv0, panel, columns = lax.optimization_barrier((inv0, panel, columns))
    with jax.named_scope("rowpanel"):
        moved, reached = send(panel, 1, last, cols)
    low1, inv1, diag1 = call(
        second_kernel, "factor_second", [(tile, wide), (tile, wide), (tile // LANES, LANES)],
        [(tile, tile)] * 3, diag, inv0,
    )

    is_new = jnp.zeros((), bool)
    for target in reached:
        is_new = is_new | (col == target)
    ids = jnp.stack([row, col, is_new.astype(jnp.int32)])
    factored, solved, site = call(
        finish_kernel, "finish", [(tile, wide), (nrhs, tile), (1, nrhs)], [(tile, wide)],
        panel, moved, columns, low0, inv0, diag0, low1, inv1, diag1, covariance, observations,
        ids=ids,
    )
    return factored, solved, site.reshape(nrhs)


def solution(mesh):
    in_specs = (P("row", "col"), P(None, "row"))
    out_specs = (P("row", "col"), P(None, "row"), P())
    return jax.shard_map(shards, mesh=mesh, in_specs=in_specs, out_specs=out_specs, check_vma=False)
```

```python
import jax
import jax.numpy as jnp
from jax import lax
from jax.experimental import pallas as pl
from jax.experimental.pallas import tpu as pltpu
from jax.sharding import PartitionSpec as P

HI = lax.Precision.HIGHEST
SUB = 8
GROUP = 4
LANES = 128
VMEM = pl.BlockSpec(memory_space=pltpu.VMEM)


def dot(a, b):
    return jnp.dot(a, b, precision=HI, preferred_element_type=jnp.float32)


def dot_t(a, b):
    dims = (((1,), (1,)), ((), ()))
    return lax.dot_general(a, b, dims, precision=HI, preferred_element_type=jnp.float32)


def factor_tile(blocks):
    shape = (SUB, LANES)
    lane = lax.broadcasted_iota(jnp.int32, shape, 1)
    sub = lax.broadcasted_iota(jnp.int32, shape, 0)
    count = len(blocks)
    blocks = list(blocks)
    upper, inverse, left, right = [], [], [], []
    for b in range(count):
        base = b * SUB
        start = b // GROUP * GROUP
        stop = start + GROUP
        here = blocks[b]
        across = [jnp.broadcast_to(here[:, base + k : base + k + 1], shape) for k in range(SUB)]
        rows = [jnp.broadcast_to(here[k : k + 1, :], shape) for k in range(SUB)]
        s = {}
        for k in range(SUB):
            for i in range(k, SUB):
                s[i, k] = jnp.broadcast_to(across[k][i : i + 1, :], shape)
        rinv, low, u, w = [], {}, [], []
        for k in range(SUB):
            rinv.append(lax.rsqrt(s[k, k]))
            for i in range(k + 1, SUB):
                low[i, k] = s[i, k] * rinv[k]
            for j in range(k + 1, SUB):
                for i in range(j, SUB):
                    s[i, j] = s[i, j] - low[i, k] * low[j, k]
            uk = rows[k]
            wk = jnp.where(lane < base, rows[k], jnp.where(lane == base + k, 1.0, 0.0))
            for m in range(k):
                uk = uk - low[k, m] * u[m]
                wk = wk - low[k, m] * w[m]
            u.append(uk * rinv[k])
            w.append(wk * rinv[k])
        u_block, w_block = u[0], w[0]
        for k in range(1, SUB):
            u_block = jnp.where(sub == k, u[k], u_block)
            w_block = jnp.where(sub == k, w[k], w_block)
        upper.append(jnp.where(lane >= sub + base, u_block, 0.0))
        inverse.append(w_block)
        left.append(u_block)
        right.append(jnp.where(lane < stop * SUB, w_block, u_block))
        if b + 1 == stop:
            if stop < count:
                far = lax.dot_general(
                    jnp.concatenate(left[start:], axis=0), jnp.concatenate(right[start:], axis=0),
                    (((0,), (0,)), ((), ())), precision=HI, preferred_element_type=jnp.float32,
                )
                keep = (lane < start * SUB) | (lane >= stop * SUB)
                for i in range(stop, count):
                    blocks[i] = jnp.where(keep, blocks[i], 0.0) - far[i * SUB : (i + 1) * SUB]
            continue
        q = [None] * SUB
        for k in reversed(range(SUB)):
            v = jnp.where(lane < base + SUB, w[k], u[k])
            for m in range(k + 1, SUB):
                v = v - low[m, k] * q[m]
            q[k] = v * rinv[k]
        keep = (lane < base) | (lane >= base + SUB)
        for i in range(b + 1, stop):
            old = blocks[i]
            terms = [
                jnp.broadcast_to(old[:, base + k : base + k + 1], shape) * q[k] for k in range(SUB)
            ]
            while len(terms) > 1:
                terms = [terms[t] + terms[t + 1] for t in range(0, len(terms), 2)]
            blocks[i] = jnp.where(keep, old, 0.0) - terms[0]
    return upper, inverse


def eliminate(work, low_ref, inv_ref, diag_ref):
    size = work.shape[0]
    row_id = lax.broadcasted_iota(jnp.int32, (size, LANES), 0)
    col_id = lax.broadcasted_iota(jnp.int32, (LANES, size), 1)
    square = (LANES, LANES)
    on_diag = lax.broadcasted_iota(jnp.int32, square, 0) == lax.broadcasted_iota(
        jnp.int32, square, 1
    )

    def step(t, carry):
        base = pl.multiple_of(t * LANES, LANES)
        tile_rows = pl.ds(base, LANES)
        here = [work[pl.ds(base + SUB * i, SUB), tile_rows] for i in range(LANES // SUB)]
        up, inv = factor_tile(here)
        up = jnp.concatenate(up, axis=0)
        inv = jnp.concatenate(inv, axis=0)
        diag_ref[pl.ds(t, 1), :] = jnp.sum(jnp.where(on_diag, up, 0.0), axis=0, keepdims=True)
        across = dot(inv, work[tile_rows, :])
        below = dot_t(work[:, tile_rows], inv)
        below = jnp.where(row_id >= base + LANES, below, 0.0)
        low_ref[:, tile_rows] = below
        low_ref[tile_rows, tile_rows] = up.T
        inv_ref[tile_rows, :] = jnp.where(col_id < base, across, 0.0)
        inv_ref[tile_rows, tile_rows] = inv
        work[tile_rows, :] = across
        work[tile_rows, tile_rows] = inv
        across = work[tile_rows, :]
        work[:, tile_rows] = jnp.zeros((size, LANES), jnp.float32)
        work[...] = work[...] - dot(below, across)
        return carry

    lax.fori_loop(0, size // LANES, step, 0)


def first_kernel(d_ref, low_ref, inv_ref, diag_ref, work):
    tile = work.shape[0]
    work[...] = d_ref[:, :tile]
    eliminate(work, low_ref, inv_ref, diag_ref)


def second_kernel(d_ref, inv0_ref, low_ref, inv_ref, diag_ref, work, low_here, inv_here):
    tile = inv0_ref.shape[0]
    inv0 = inv0_ref[...]
    left = dot_t(d_ref[:, tile : 2 * tile], inv0)
    low_ref[:, :tile] = left
    work[...] = d_ref[:, 2 * tile : 3 * tile] - dot_t(left, left)
    eliminate(work, low_here, inv_here, diag_ref)
    low_ref[:, tile:] = low_here[...]
    inv1 = inv_here[...]
    inv_ref[:, tile:] = inv1
    inv_ref[:, :tile] = -dot(inv1, dot(low_ref[:, :tile], inv0))


def finish_kernel(
    ids_ref, panel_ref, moved_ref, wide_ref, low0_ref, inv0_ref, diag0_ref, low1_ref, inv1_ref,
    diag1_ref, cov_ref, obs_ref, out_ref, solved_ref, site_ref, rows_here,
):
    tile, wide = cov_ref.shape
    nrhs = obs_ref.shape[0]
    row, col, is_new = ids_ref[0], ids_ref[1], ids_ref[2]
    inv0 = inv0_ref[...]
    inv10 = inv1_ref[:, :tile]
    inv11 = inv1_ref[:, tile:]

    rows_here[...] = panel_ref[...]

    @pl.when(is_new == 1)
    def _():
        rows_here[...] = moved_ref[...]

    obs_both = wide_ref[:, 2 * wide : 2 * wide + 2 * nrhs]
    z0 = dot(inv0, obs_both)[:, :nrhs]
    z1 = dot(inv10, obs_both)[:, :nrhs] + dot(inv11, obs_both)[:, nrhs:]
    quad = jnp.sum(z0 * z0 + z1 * z1, axis=0, keepdims=True)
    logs = jnp.log(diag0_ref[...]) + jnp.log(diag1_ref[...])
    site_ref[...] = -(quad + 2.0 * jnp.sum(logs)) / (4.0 * tile)

    @pl.when(row == 0)
    def _():
        solved_ref[...] = z0.T

    @pl.when(row == 1)
    def _():
        solved_ref[...] = z1.T

    @pl.when(row <= 1)
    def _():
        out_ref[...] = jnp.zeros((tile, wide), jnp.float32)

    @pl.when((row == 0) & (col == 0))
    def _():
        out_ref[:, :tile] = low0_ref[...]

    @pl.when((row == 1) & (col == 0))
    def _():
        out_ref[...] = low1_ref[...]

    @pl.when(row > 1)
    def _():
        x0 = dot_t(rows_here[:, :tile], inv0)
        x1 = dot_t(rows_here[...], inv1_ref[...])
        solved_ref[...] = obs_ref[...] - (dot(x0, z0) + dot(x1, z1)).T

        @pl.when(col == 0)
        def _():
            out_ref[:, :tile] = x0
            out_ref[:, tile:] = x1

        @pl.when(col > 0)
        def _():
            c0 = wide_ref[:, :wide]
            y0 = dot(inv0, c0)
            y1 = dot(inv10, c0) + dot(inv11, wide_ref[:, wide : 2 * wide])
            out_ref[...] = cov_ref[...] - dot(x0, y0) - dot(x1, y1)


def call(kernel, name, outs, scratch, *args, ids=None):
    flops = 4 * 256**3
    specs = [VMEM] * len(args)
    if ids is not None:
        specs = [pl.BlockSpec(memory_space=pltpu.SMEM)] + specs
        args = (ids,) + args
    return pl.pallas_call(
        kernel,
        out_shape=[jax.ShapeDtypeStruct(shape, jnp.float32) for shape in outs],
        in_specs=specs,
        out_specs=[VMEM] * len(outs),
        scratch_shapes=[pltpu.VMEM(shape, jnp.float32) for shape in scratch],
        compiler_params=pltpu.CompilerParams(vmem_limit_bytes=16 * 1024 * 1024),
        cost_estimate=pl.CostEstimate(flops=flops, bytes_accessed=40 * 2**20, transcendentals=0),
        name=name,
    )(*args)


def send(value, hop, holders, extent):
    pairs = [(z, (z + hop) % extent) for z in holders]
    return lax.ppermute(value, "col", pairs), [target for _, target in pairs]


def pick(value, moved, targets, position):
    is_new = jnp.zeros((), bool)
    for target in targets:
        is_new = is_new | (position == target)
    return jnp.where(is_new, moved, value)


def spread_step(value, hops, holders, extent, position):
    arrived, targets = None, []
    for hop in hops:
        moved, reached = send(value, hop, holders, extent)
        arrived = moved if arrived is None else arrived + moved
        targets += reached
    is_new = jnp.zeros((), bool)
    for target in targets:
        is_new = is_new | (position == target)
    return jnp.where(is_new, arrived, value), sorted(set(holders) | set(targets))


def shards(covariance, observations):
    tile, wide = covariance.shape
    nrhs = observations.shape[0]
    rows = lax.axis_size("row")
    cols = lax.axis_size("col")
    row = lax.axis_index("row")
    col = lax.axis_index("col")
    part = tile // rows

    def exchange(value):
        return lax.all_to_all(value, "row", split_axis=0, concat_axis=0, tiled=True)

    with jax.named_scope("scatter"):
        got = exchange(covariance.reshape(rows, part, wide))
        first, second = got[0], got[1]
        obs_parts = jnp.pad(observations.T, ((0, 0), (0, LANES - nrhs))).reshape(rows, part, LANES)

    with jax.named_scope("diag"):
        piece = jnp.concatenate([first[:, :tile], second], axis=1)
        near, reached = send(piece, 5, [0], cols)
        piece, near, reached = pick(piece, near, reached, col), piece, [0] + reached
        back, backs = send(piece, -2, reached, cols)
        ahead, aheads = send(piece, 2, reached, cols)
        near, piece = lax.optimization_barrier((near, piece))
        far, fars = send(near, -5, [0], cols)
        piece = pick(piece, far, fars, col)
        far_back, far_backs = send(piece, -2, fars, cols)
        far_ahead, far_aheads = send(piece, 2, fars, cols)
        piece = pick(pick(piece, back, backs, col), ahead, aheads, col)
        piece = pick(pick(piece, far_back, far_backs, col), far_ahead, far_aheads, col)
        last = [z for z in range(cols) if z in reached + backs + aheads + fars + far_backs + far_aheads]
        last = [z for z in last if (z + 1) % cols not in last]
        piece, _ = spread_step(piece, (1,), last, cols, col)
        panel, piece = lax.optimization_barrier((covariance, piece))
        sent = jnp.broadcast_to(piece[None], (rows,) + piece.shape)
        whole = exchange(jnp.concatenate([sent, obs_parts], axis=2))
        diag = whole.reshape(tile, -1)

    with jax.named_scope("columns"):
        start = 3 * tile
        col_piece = jnp.concatenate(
            [first, second, whole[0, :, start : start + nrhs], whole[1, :, start : start + nrhs]],
            axis=1,
        )
        columns = exchange(jnp.broadcast_to(col_piece[None], (rows,) + col_piece.shape))
        columns = columns.reshape(tile, -1)

    with jax.named_scope("rowpanel"):
        panel, holders = spread_step(panel, (-5, 5), [0], cols, col)
        panel, holders = spread_step(panel, (2, -2), holders, cols, col)

    low0, inv0, diag0 = call(
        first_kernel, "factor_first", [(tile, tile), (tile, tile), (tile // LANES, LANES)],
        [(tile, tile)], diag,
    )
    inv0, panel, columns = lax.optimization_barrier((inv0, panel, columns))
    with jax.named_scope("rowpanel"):
        moved, reached = send(panel, 1, last, cols)
    low1, inv1, diag1 = call(
        second_kernel, "factor_second", [(tile, wide), (tile, wide), (tile // LANES, LANES)],
        [(tile, tile)] * 3, diag, inv0,
    )

    is_new = jnp.zeros((), bool)
    for target in reached:
        is_new = is_new | (col == target)
    ids = jnp.stack([row, col, is_new.astype(jnp.int32)])
    factored, solved, site = call(
        finish_kernel, "finish", [(tile, wide), (nrhs, tile), (1, nrhs)], [(tile, wide)],
        panel, moved, columns, low0, inv0, diag0, low1, inv1, diag1, covariance, observations,
        ids=ids,
    )
    return factored, solved, site.reshape(nrhs)


def solution(mesh):
    in_specs = (P("row", "col"), P(None, "row"))
    out_specs = (P("row", "col"), P(None, "row"), P())
    return jax.shard_map(shards, mesh=mesh, in_specs=in_specs, out_specs=out_specs, check_vma=False)
```

```python
import jax
import jax.numpy as jnp
from jax import lax
from jax.experimental import pallas as pl
from jax.experimental.pallas import tpu as pltpu
from jax.sharding import PartitionSpec as P

HI = lax.Precision.HIGHEST
SUB = 8
GROUP = 4
LANES = 128
VMEM = pl.BlockSpec(memory_space=pltpu.VMEM)


def dot(a, b):
    return jnp.dot(a, b, precision=HI, preferred_element_type=jnp.float32)


def dot_t(a, b):
    dims = (((1,), (1,)), ((), ()))
    return lax.dot_general(a, b, dims, precision=HI, preferred_element_type=jnp.float32)


def split(value):
    high = value.astype(jnp.bfloat16)
    rest = value - high.astype(jnp.float32)
    middle = rest.astype(jnp.bfloat16)
    low = (rest - middle.astype(jnp.float32)).astype(jnp.bfloat16)
    return high, middle, low


def outer_sum(left, right):
    a1, a2, a3 = split(jnp.concatenate(left, axis=0))
    b1, b2, b3 = split(jnp.concatenate(right, axis=0))
    a = jnp.concatenate([a1, a1, a2, a1, a2, a3], axis=0)
    b = jnp.concatenate([b1, b2, b1, b3, b2, b1], axis=0)
    dims = (((0,), (0,)), ((), ()))
    return lax.dot_general(a, b, dims, preferred_element_type=jnp.float32)


def factor_tile(blocks):
    shape = (SUB, LANES)
    lane = lax.broadcasted_iota(jnp.int32, shape, 1)
    sub = lax.broadcasted_iota(jnp.int32, shape, 0)
    count = len(blocks)
    blocks = list(blocks)
    upper, inverse, left, right = [], [], [], []
    for b in range(count):
        base = b * SUB
        start = b // GROUP * GROUP
        stop = start + GROUP
        here = blocks[b]
        across = [jnp.broadcast_to(here[:, base + k : base + k + 1], shape) for k in range(SUB)]
        rows = [jnp.broadcast_to(here[k : k + 1, :], shape) for k in range(SUB)]
        s = {}
        for k in range(SUB):
            for i in range(k, SUB):
                s[i, k] = jnp.broadcast_to(across[k][i : i + 1, :], shape)
        rinv, low, u, w = [], {}, [], []
        for k in range(SUB):
            rinv.append(lax.rsqrt(s[k, k]))
            for i in range(k + 1, SUB):
                low[i, k] = s[i, k] * rinv[k]
            for j in range(k + 1, SUB):
                for i in range(j, SUB):
                    s[i, j] = s[i, j] - low[i, k] * low[j, k]
            uk = rows[k]
            wk = jnp.where(lane < base, rows[k], jnp.where(lane == base + k, 1.0, 0.0))
            for m in range(k):
                uk = uk - low[k, m] * u[m]
                wk = wk - low[k, m] * w[m]
            u.append(uk * rinv[k])
            w.append(wk * rinv[k])
        u_block, w_block = u[0], w[0]
        for k in range(1, SUB):
            u_block = jnp.where(sub == k, u[k], u_block)
            w_block = jnp.where(sub == k, w[k], w_block)
        upper.append(jnp.where(lane >= sub + base, u_block, 0.0))
        inverse.append(w_block)
        left.append(u_block)
        right.append(jnp.where(lane < stop * SUB, w_block, u_block))
        if b + 1 == stop:
            if stop < count:
                far = outer_sum(left[start:], right[start:])
                keep = (lane < start * SUB) | (lane >= stop * SUB)
                for i in range(stop, count):
                    blocks[i] = jnp.where(keep, blocks[i], 0.0) - far[i * SUB : (i + 1) * SUB]
            continue
        q = [None] * SUB
        for k in reversed(range(SUB)):
            v = jnp.where(lane < base + SUB, w[k], u[k])
            for m in range(k + 1, SUB):
                v = v - low[m, k] * q[m]
            q[k] = v * rinv[k]
        keep = (lane < base) | (lane >= base + SUB)
        for i in range(b + 1, stop):
            old = blocks[i]
            terms = [
                jnp.broadcast_to(old[:, base + k : base + k + 1], shape) * q[k] for k in range(SUB)
            ]
            while len(terms) > 1:
                terms = [terms[t] + terms[t + 1] for t in range(0, len(terms), 2)]
            blocks[i] = jnp.where(keep, old, 0.0) - terms[0]
    return upper, inverse


def eliminate(corner, below, last, low_ref, inv_ref, diag_ref, tile_here, mid_here):
    square = (LANES, LANES)
    on_diag = lax.broadcasted_iota(jnp.int32, square, 0) == lax.broadcasted_iota(
        jnp.int32, square, 1
    )
    zero = jnp.zeros(square, jnp.float32)
    low_ref[:LANES, LANES:] = zero
    inv_ref[:LANES, LANES:] = zero
    tile_here[...] = corner()

    def step(t, carry):
        tile_rows = pl.ds(pl.multiple_of(t * LANES, LANES), LANES)
        up, inv = factor_tile(
            [tile_here[SUB * i : SUB * (i + 1), :] for i in range(LANES // SUB)]
        )
        up = jnp.concatenate(up, axis=0)
        inv = jnp.concatenate(inv, axis=0)
        diag_ref[pl.ds(t, 1), :] = jnp.sum(jnp.where(on_diag, up, 0.0), axis=0, keepdims=True)
        low_ref[tile_rows, tile_rows] = up.T
        inv_ref[tile_rows, tile_rows] = inv

        @pl.when(t == 0)
        def _():
            left = dot_t(below(), inv)
            low_ref[LANES:, :LANES] = left
            tile_here[...] = last() - dot_t(left, left)
            mid_here[...] = dot(left, inv)

        @pl.when(t == 1)
        def _():
            inv_ref[LANES:, :LANES] = -dot(inv, mid_here[...])

        return carry

    lax.fori_loop(0, 2, step, 0)


def first_kernel(d_ref, both_ref, diag_ref, tile_here, mid_here):
    size = 2 * LANES
    eliminate(
        lambda: d_ref[:LANES, :LANES], lambda: d_ref[LANES:, :LANES],
        lambda: d_ref[LANES:, LANES:size], both_ref.at[:, :size], both_ref.at[:, size:],
        diag_ref, tile_here, mid_here,
    )


def second_kernel(
    d_ref, both0_ref, low_ref, inv_ref, diag_ref, work, low_here, inv_here, tile_here, mid_here
):
    tile = work.shape[0]
    inv0 = both0_ref[:, tile:]
    left = dot_t(d_ref[:, tile : 2 * tile], inv0)
    low_ref[:, :tile] = left
    work[...] = d_ref[:, 2 * tile : 3 * tile] - dot_t(left, left)
    eliminate(
        lambda: work[:LANES, :LANES], lambda: work[LANES:, :LANES], lambda: work[LANES:, LANES:],
        low_here, inv_here, diag_ref, tile_here, mid_here,
    )
    low_ref[:, tile:] = low_here[...]
    inv1 = inv_here[...]
    inv_ref[:, tile:] = inv1
    inv_ref[:, :tile] = -dot(inv1, dot(low_ref[:, :tile], inv0))


def finish_kernel(
    ids_ref, panel_ref, moved_ref, wide_ref, both0_ref, diag0_ref, low1_ref, inv1_ref,
    diag1_ref, cov_ref, obs_ref, out_ref, solved_ref, site_ref, rows_here,
):
    tile, wide = cov_ref.shape
    nrhs = obs_ref.shape[0]
    row, col, is_new = ids_ref[0], ids_ref[1], ids_ref[2]
    inv0 = both0_ref[:, tile:]
    inv10 = inv1_ref[:, :tile]
    inv11 = inv1_ref[:, tile:]

    rows_here[...] = panel_ref[...]

    @pl.when(is_new == 1)
    def _():
        rows_here[...] = moved_ref[...]

    obs_both = wide_ref[:, 2 * wide : 2 * wide + 2 * nrhs]
    z0 = dot(inv0, obs_both)[:, :nrhs]
    z1 = dot(inv10, obs_both)[:, :nrhs] + dot(inv11, obs_both)[:, nrhs:]
    quad = jnp.sum(z0 * z0 + z1 * z1, axis=0, keepdims=True)
    logs = jnp.log(diag0_ref[...]) + jnp.log(diag1_ref[...])
    site_ref[...] = -(quad + 2.0 * jnp.sum(logs)) / (4.0 * tile)

    @pl.when(row == 0)
    def _():
        solved_ref[...] = z0.T

    @pl.when(row == 1)
    def _():
        solved_ref[...] = z1.T

    @pl.when(row <= 1)
    def _():
        out_ref[...] = jnp.zeros((tile, wide), jnp.float32)

    @pl.when((row == 0) & (col == 0))
    def _():
        out_ref[:, :tile] = both0_ref[:, :tile]

    @pl.when((row == 1) & (col == 0))
    def _():
        out_ref[...] = low1_ref[...]

    @pl.when(row > 1)
    def _():
        x0 = dot_t(rows_here[:, :tile], inv0)
        x1 = dot_t(rows_here[...], inv1_ref[...])
        solved_ref[...] = obs_ref[...] - (dot(x0, z0) + dot(x1, z1)).T

        @pl.when(col == 0)
        def _():
            out_ref[:, :tile] = x0
            out_ref[:, tile:] = x1

        @pl.when(col > 0)
        def _():
            c0 = wide_ref[:, :wide]
            y0 = dot(inv0, c0)
            y1 = dot(inv10, c0) + dot(inv11, wide_ref[:, wide : 2 * wide])
            out_ref[...] = cov_ref[...] - dot(x0, y0) - dot(x1, y1)


def call(kernel, name, outs, scratch, *args, ids=None):
    flops = 4 * 256**3
    specs = [VMEM] * len(args)
    if ids is not None:
        specs = [pl.BlockSpec(memory_space=pltpu.SMEM)] + specs
        args = (ids,) + args
    return pl.pallas_call(
        kernel,
        out_shape=[jax.ShapeDtypeStruct(shape, jnp.float32) for shape in outs],
        in_specs=specs,
        out_specs=[VMEM] * len(outs),
        scratch_shapes=[pltpu.VMEM(shape, jnp.float32) for shape in scratch],
        compiler_params=pltpu.CompilerParams(vmem_limit_bytes=16 * 1024 * 1024),
        cost_estimate=pl.CostEstimate(flops=flops, bytes_accessed=40 * 2**20, transcendentals=0),
        name=name,
    )(*args)


def send(value, hop, holders, extent):
    pairs = [(z, (z + hop) % extent) for z in holders]
    return lax.ppermute(value, "col", pairs), [target for _, target in pairs]


def pick(value, moved, targets, position):
    is_new = jnp.zeros((), bool)
    for target in targets:
        is_new = is_new | (position == target)
    return jnp.where(is_new, moved, value)


def spread_step(value, hops, holders, extent, position):
    sent = [send(value, hop, holders, extent) for hop in hops]
    reached = set(holders)
    for moved, targets in sent:
        value = pick(value, moved, targets, position)
        reached |= set(targets)
    return value, sorted(reached)


def shards(covariance, observations):
    tile, wide = covariance.shape
    nrhs = observations.shape[0]
    rows = lax.axis_size("row")
    cols = lax.axis_size("col")
    row = lax.axis_index("row")
    col = lax.axis_index("col")
    part = tile // rows

    def exchange(value):
        return lax.all_to_all(value, "row", split_axis=0, concat_axis=0, tiled=True)

    with jax.named_scope("scatter"):
        got = exchange(covariance.reshape(rows, part, wide))
        first, second = got[0], got[1]
        obs_parts = jnp.pad(observations.T, ((0, 0), (0, LANES - nrhs))).reshape(rows, part, LANES)

    with jax.named_scope("diag"):
        piece = jnp.concatenate([first[:, :tile], second], axis=1)
        near, reached = send(piece, 5, [0], cols)
        piece, near, reached = pick(piece, near, reached, col), piece, [0] + reached
        back, backs = send(piece, -2, reached, cols)
        ahead, aheads = send(piece, 2, reached, cols)
        near, piece = lax.optimization_barrier((near, piece))
        far, fars = send(near, -5, [0], cols)
        piece = pick(piece, far, fars, col)
        far_back, far_backs = send(piece, -2, fars, cols)
        far_ahead, far_aheads = send(piece, 2, fars, cols)
        piece = pick(pick(piece, back, backs, col), ahead, aheads, col)
        piece = pick(pick(piece, far_back, far_backs, col), far_ahead, far_aheads, col)
        last = [z for z in range(cols) if z in reached + backs + aheads + fars + far_backs + far_aheads]
        last = [z for z in last if (z + 1) % cols not in last]
        piece, _ = spread_step(piece, (1,), last, cols, col)
        panel, piece = lax.optimization_barrier((covariance, piece))
        sent = jnp.broadcast_to(piece[None], (rows,) + piece.shape)
        whole = exchange(jnp.concatenate([sent, obs_parts], axis=2))
        diag = whole.reshape(tile, -1)

    with jax.named_scope("columns"):
        start = 3 * tile
        col_piece = jnp.concatenate(
            [first, second, whole[0, :, start : start + nrhs], whole[1, :, start : start + nrhs]],
            axis=1,
        )
        columns = exchange(jnp.broadcast_to(col_piece[None], (rows,) + col_piece.shape))
        columns = columns.reshape(tile, -1)

    with jax.named_scope("rowpanel"):
        panel, holders = spread_step(panel, (5, -5), [0], cols, col)
        panel, holders = spread_step(panel, (-2, 2), holders, cols, col)

    square = (LANES, LANES)
    both0, diag0 = call(
        first_kernel, "factor_first", [(tile, wide), (tile // LANES, LANES)], [square] * 2, diag
    )
    both0, panel, columns = lax.optimization_barrier((both0, panel, columns))
    with jax.named_scope("rowpanel"):
        moved, reached = send(panel, 1, last, cols)
    low1, inv1, diag1 = call(
        second_kernel, "factor_second", [(tile, wide), (tile, wide), (tile // LANES, LANES)],
        [(tile, tile)] * 3 + [square] * 2, diag, both0,
    )

    is_new = jnp.zeros((), bool)
    for target in reached:
        is_new = is_new | (col == target)
    ids = jnp.stack([row, col, is_new.astype(jnp.int32)])
    factored, solved, site = call(
        finish_kernel, "finish", [(tile, wide), (nrhs, tile), (1, nrhs)], [(tile, wide)],
        panel, moved, columns, both0, diag0, low1, inv1, diag1, covariance, observations,
        ids=ids,
    )
    return factored, solved, site.reshape(nrhs)


def solution(mesh):
    in_specs = (P("row", "col"), P(None, "row"))
    out_specs = (P("row", "col"), P(None, "row"), P())
    return jax.shard_map(shards, mesh=mesh, in_specs=in_specs, out_specs=out_specs, check_vma=False)
```

```python
import jax
import jax.numpy as jnp
from jax import lax
from jax.experimental import pallas as pl
from jax.experimental.pallas import tpu as pltpu
from jax.sharding import PartitionSpec as P

HI = lax.Precision.HIGHEST
SUB = 8
GROUP = 4
LANES = 128
VMEM = pl.BlockSpec(memory_space=pltpu.VMEM)


def dot(a, b):
    return jnp.dot(a, b, precision=HI, preferred_element_type=jnp.float32)


def dot_t(a, b):
    dims = (((1,), (1,)), ((), ()))
    return lax.dot_general(a, b, dims, precision=HI, preferred_element_type=jnp.float32)


def split(value):
    high = value.astype(jnp.bfloat16)
    rest = value - high.astype(jnp.float32)
    middle = rest.astype(jnp.bfloat16)
    low = (rest - middle.astype(jnp.float32)).astype(jnp.bfloat16)
    return high, middle, low


def outer_sum(left, right):
    a1, a2, a3 = split(jnp.concatenate(left, axis=0))
    b1, b2, b3 = split(jnp.concatenate(right, axis=0))
    a = jnp.concatenate([a1, a1, a2, a1, a2, a3], axis=0)
    b = jnp.concatenate([b1, b2, b1, b3, b2, b1], axis=0)
    dims = (((0,), (0,)), ((), ()))
    return lax.dot_general(a, b, dims, preferred_element_type=jnp.float32)


def factor_tile(blocks):
    shape = (SUB, LANES)
    lane = lax.broadcasted_iota(jnp.int32, shape, 1)
    sub = lax.broadcasted_iota(jnp.int32, shape, 0)
    count = len(blocks)
    blocks = list(blocks)
    upper, inverse, left, right = [], [], [], []
    for b in range(count):
        base = b * SUB
        start = b // GROUP * GROUP
        stop = start + GROUP
        here = blocks[b]
        across = [jnp.broadcast_to(here[:, base + k : base + k + 1], shape) for k in range(SUB)]
        rows = [jnp.broadcast_to(here[k : k + 1, :], shape) for k in range(SUB)]
        s = {}
        for k in range(SUB):
            for i in range(k, SUB):
                s[i, k] = jnp.broadcast_to(across[k][i : i + 1, :], shape)
        rinv, low, u, w = [], {}, [], []
        for k in range(SUB):
            rinv.append(lax.rsqrt(s[k, k]))
            for i in range(k + 1, SUB):
                low[i, k] = s[i, k] * rinv[k]
            for j in range(k + 1, SUB):
                for i in range(j, SUB):
                    s[i, j] = s[i, j] - low[i, k] * low[j, k]
            uk = rows[k]
            wk = jnp.where(lane < base, rows[k], jnp.where(lane == base + k, 1.0, 0.0))
            for m in range(k):
                uk = uk - low[k, m] * u[m]
                wk = wk - low[k, m] * w[m]
            u.append(uk * rinv[k])
            w.append(wk * rinv[k])
        u_block, w_block = u[0], w[0]
        for k in range(1, SUB):
            u_block = jnp.where(sub == k, u[k], u_block)
            w_block = jnp.where(sub == k, w[k], w_block)
        upper.append(jnp.where(lane >= sub + base, u_block, 0.0))
        inverse.append(w_block)
        left.append(u_block)
        right.append(jnp.where(lane < stop * SUB, w_block, u_block))
        if b + 1 == stop:
            if stop < count:
                far = outer_sum(left[start:], right[start:])
                keep = (lane < start * SUB) | (lane >= stop * SUB)
                for i in range(stop, count):
                    blocks[i] = jnp.where(keep, blocks[i], 0.0) - far[i * SUB : (i + 1) * SUB]
            continue
        q = [None] * SUB
        for k in reversed(range(SUB)):
            v = jnp.where(lane < base + SUB, w[k], u[k])
            for m in range(k + 1, SUB):
                v = v - low[m, k] * q[m]
            q[k] = v * rinv[k]
        keep = (lane < base) | (lane >= base + SUB)
        for i in range(b + 1, stop):
            old = blocks[i]
            terms = [
                jnp.broadcast_to(old[:, base + k : base + k + 1], shape) * q[k] for k in range(SUB)
            ]
            while len(terms) > 1:
                terms = [terms[t] + terms[t + 1] for t in range(0, len(terms), 2)]
            blocks[i] = jnp.where(keep, old, 0.0) - terms[0]
    return upper, inverse


def eliminate(corner, below, last, low_ref, inv_ref, diag_ref, tile_here, mid_here):
    square = (LANES, LANES)
    on_diag = lax.broadcasted_iota(jnp.int32, square, 0) == lax.broadcasted_iota(
        jnp.int32, square, 1
    )
    zero = jnp.zeros(square, jnp.float32)
    low_ref[:LANES, LANES:] = zero
    inv_ref[:LANES, LANES:] = zero
    tile_here[...] = corner()

    def step(t, carry):
        tile_rows = pl.ds(pl.multiple_of(t * LANES, LANES), LANES)
        up, inv = factor_tile(
            [tile_here[SUB * i : SUB * (i + 1), :] for i in range(LANES // SUB)]
        )
        up = jnp.concatenate(up, axis=0)
        inv = jnp.concatenate(inv, axis=0)
        diag_ref[pl.ds(t, 1), :] = jnp.sum(jnp.where(on_diag, up, 0.0), axis=0, keepdims=True)
        low_ref[tile_rows, tile_rows] = up.T
        inv_ref[tile_rows, tile_rows] = inv

        @pl.when(t == 0)
        def _():
            left = dot_t(below(), inv)
            low_ref[LANES:, :LANES] = left
            tile_here[...] = last() - dot_t(left, left)
            mid_here[...] = dot(left, inv)

        @pl.when(t == 1)
        def _():
            inv_ref[LANES:, :LANES] = -dot(inv, mid_here[...])

        return carry

    lax.fori_loop(0, 2, step, 0)


def first_kernel(d_ref, both_ref, diag_ref, tile_here, mid_here):
    size = 2 * LANES
    eliminate(
        lambda: d_ref[:LANES, :LANES], lambda: d_ref[LANES:, :LANES],
        lambda: d_ref[LANES:, LANES:size], both_ref.at[:, :size], both_ref.at[:, size:],
        diag_ref, tile_here, mid_here,
    )


def second_kernel(
    d_ref, both0_ref, low_ref, inv_ref, diag_ref, work, low_here, inv_here, tile_here, mid_here
):
    tile = work.shape[0]
    inv0 = both0_ref[:, tile:]
    left = dot_t(d_ref[:, tile : 2 * tile], inv0)
    low_ref[:, :tile] = left
    work[...] = d_ref[:, 2 * tile : 3 * tile] - dot_t(left, left)
    eliminate(
        lambda: work[:LANES, :LANES], lambda: work[LANES:, :LANES], lambda: work[LANES:, LANES:],
        low_here, inv_here, diag_ref, tile_here, mid_here,
    )
    low_ref[:, tile:] = low_here[...]
    inv1 = inv_here[...]
    inv_ref[:, tile:] = inv1
    inv_ref[:, :tile] = -dot(inv1, dot(low_ref[:, :tile], inv0))


def parts_dot(a, b):
    a1, a2, a3 = split(a)
    b1, b2, b3 = split(b)
    a = jnp.concatenate([a1, a1, a2, a1, a2, a3], axis=1)
    b = jnp.concatenate([b1, b2, b1, b3, b2, b1], axis=0)
    return jnp.dot(a, b, preferred_element_type=jnp.float32)


def parts_dot_t(a, b):
    a1, a2, a3 = split(a)
    b1, b2, b3 = split(b)
    a = jnp.concatenate([a1, a1, a2, a1, a2, a3], axis=1)
    b = jnp.concatenate([b1, b2, b1, b3, b2, b1], axis=1)
    dims = (((1,), (1,)), ((), ()))
    return lax.dot_general(a, b, dims, preferred_element_type=jnp.float32)


def finish_kernel(
    ids_ref, panel_ref, back_ref, ahead_ref, next_ref, prior_ref, rest_ref, wide_ref, both0_ref, diag0_ref, low1_ref, inv1_ref,
    diag1_ref, cov_ref, obs_ref, out_ref, solved_ref, site_ref, rows_here,
):
    tile, wide = cov_ref.shape
    nrhs = obs_ref.shape[0]
    row, col, source = ids_ref[0], ids_ref[1], ids_ref[2]
    inv0 = both0_ref[:, tile:]
    inv10 = inv1_ref[:, :tile]
    inv11 = inv1_ref[:, tile:]

    for place, ref in enumerate([panel_ref, back_ref, ahead_ref, next_ref, prior_ref, rest_ref]):
        @pl.when(source == place)
        def _(ref=ref):
            rows_here[...] = ref[...]

    obs_both = wide_ref[:, 2 * wide : 2 * wide + 2 * nrhs]
    z0 = parts_dot(inv0, obs_both)[:, :nrhs]
    z1 = parts_dot(inv10, obs_both)[:, :nrhs] + parts_dot(inv11, obs_both)[:, nrhs:]
    quad = jnp.sum(z0 * z0 + z1 * z1, axis=0, keepdims=True)
    logs = jnp.log(diag0_ref[...]) + jnp.log(diag1_ref[...])
    site_ref[...] = -(quad + 2.0 * jnp.sum(logs)) / (4.0 * tile)

    @pl.when(row == 0)
    def _():
        solved_ref[...] = z0.T

    @pl.when(row == 1)
    def _():
        solved_ref[...] = z1.T

    @pl.when(row <= 1)
    def _():
        out_ref[...] = jnp.zeros((tile, wide), jnp.float32)

    @pl.when((row == 0) & (col == 0))
    def _():
        out_ref[:, :tile] = both0_ref[:, :tile]

    @pl.when((row == 1) & (col == 0))
    def _():
        out_ref[...] = low1_ref[...]

    @pl.when(row > 1)
    def _():
        x0 = parts_dot_t(rows_here[:, :tile], inv0)
        x1 = parts_dot_t(rows_here[...], inv1_ref[...])
        solved_ref[...] = obs_ref[...] - (parts_dot(x0, z0) + parts_dot(x1, z1)).T

        @pl.when(col == 0)
        def _():
            out_ref[:, :tile] = x0
            out_ref[:, tile:] = x1

        @pl.when(col > 0)
        def _():
            c0 = wide_ref[:, :wide]
            y0 = parts_dot(inv0, c0)
            y1 = parts_dot(inv10, c0) + parts_dot(inv11, wide_ref[:, wide : 2 * wide])
            out_ref[...] = cov_ref[...] - parts_dot(x0, y0) - parts_dot(x1, y1)


def call(kernel, name, outs, scratch, *args, ids=None):
    flops = 4 * 256**3
    specs = [VMEM] * len(args)
    if ids is not None:
        specs = [pl.BlockSpec(memory_space=pltpu.SMEM)] + specs
        args = (ids,) + args
    return pl.pallas_call(
        kernel,
        out_shape=[jax.ShapeDtypeStruct(shape, jnp.float32) for shape in outs],
        in_specs=specs,
        out_specs=[VMEM] * len(outs),
        scratch_shapes=[pltpu.VMEM(shape, jnp.float32) for shape in scratch],
        compiler_params=pltpu.CompilerParams(vmem_limit_bytes=16 * 1024 * 1024),
        cost_estimate=pl.CostEstimate(flops=flops, bytes_accessed=40 * 2**20, transcendentals=0),
        name=name,
    )(*args)


def send(value, hop, holders, extent):
    pairs = [(z, (z + hop) % extent) for z in holders]
    return lax.ppermute(value, "col", pairs), [target for _, target in pairs]


def pick(value, moved, targets, position):
    is_new = jnp.zeros((), bool)
    for target in targets:
        is_new = is_new | (position == target)
    return jnp.where(is_new, moved, value)


def spread_step(value, hops, holders, extent, position):
    sent = [send(value, hop, holders, extent) for hop in hops]
    reached = set(holders)
    for moved, targets in sent:
        value = pick(value, moved, targets, position)
        reached |= set(targets)
    return value, sorted(reached)


def shards(covariance, observations):
    tile, wide = covariance.shape
    nrhs = observations.shape[0]
    rows = lax.axis_size("row")
    cols = lax.axis_size("col")
    row = lax.axis_index("row")
    col = lax.axis_index("col")
    part = tile // rows

    def exchange(value):
        return lax.all_to_all(value, "row", split_axis=0, concat_axis=0, tiled=True)

    with jax.named_scope("scatter"):
        got = exchange(covariance.reshape(rows, part, wide))
        first, second = got[0], got[1]
        obs_parts = jnp.pad(observations.T, ((0, 0), (0, LANES - nrhs))).reshape(rows, part, LANES)

    with jax.named_scope("diag"):
        piece = jnp.concatenate([first[:, :tile], second], axis=1)
        near, reached = send(piece, 5, [0], cols)
        piece, near, reached = pick(piece, near, reached, col), piece, [0] + reached
        back, backs = send(piece, -2, reached, cols)
        ahead, aheads = send(piece, 2, reached, cols)
        near, piece = lax.optimization_barrier((near, piece))
        far, fars = send(near, -5, [0], cols)
        piece = pick(piece, far, fars, col)
        far_back, far_backs = send(piece, -2, fars, cols)
        far_ahead, far_aheads = send(piece, 2, fars, cols)
        piece = pick(pick(piece, back, backs, col), ahead, aheads, col)
        piece = pick(pick(piece, far_back, far_backs, col), far_ahead, far_aheads, col)
        last = [z for z in range(cols) if z in reached + backs + aheads + fars + far_backs + far_aheads]
        last = [z for z in last if (z + 1) % cols not in last]
        piece, _ = spread_step(piece, (1,), last, cols, col)
        panel, piece = lax.optimization_barrier((covariance, piece))
        sent = jnp.broadcast_to(piece[None], (rows,) + piece.shape)
        whole = exchange(jnp.concatenate([sent, obs_parts], axis=2))
        diag = whole.reshape(tile, -1)

    with jax.named_scope("columns"):
        start = 3 * tile
        col_piece = jnp.concatenate(
            [first, second, whole[0, :, start : start + nrhs], whole[1, :, start : start + nrhs]],
            axis=1,
        )
        columns = exchange(jnp.broadcast_to(col_piece[None], (rows,) + col_piece.shape))
        columns = columns.reshape(tile, -1)

    with jax.named_scope("rowpanel"):
        panel, holders = spread_step(panel, (5, -5), [0], cols, col)
        sends = [send(panel, hop, holders, cols) for hop in (-2, 2)]

    square = (LANES, LANES)
    both0, diag0 = call(
        first_kernel, "factor_first", [(tile, wide), (tile // LANES, LANES)], [square] * 2, diag
    )
    both0, panel, columns = lax.optimization_barrier((both0, panel, columns))
    with jax.named_scope("rowpanel"):
        sends += [send(panel, hop, holders, cols) for hop in (1, -1)]
        back, backs = sends[0]
        covered = set(holders).union(*[targets for _, targets in sends])
        rest = [z for z in backs if (z - 1) % cols not in covered]
        sends.append(send(back, -1, rest, cols))
    low1, inv1, diag1 = call(
        second_kernel, "factor_second", [(tile, wide), (tile, wide), (tile // LANES, LANES)],
        [(tile, tile)] * 3 + [square] * 2, diag, both0,
    )

    source = jnp.zeros((), jnp.int32)
    for place, (_, targets) in enumerate(sends):
        for target in targets:
            source = jnp.where(col == target, place + 1, source)
    ids = jnp.stack([row, col, source])
    factored, solved, site = call(
        finish_kernel, "finish", [(tile, wide), (nrhs, tile), (1, nrhs)], [(tile, wide)],
        panel, *[moved for moved, _ in sends], columns, both0, diag0, low1, inv1, diag1, covariance, observations,
        ids=ids,
    )
    return factored, solved, site.reshape(nrhs)


def solution(mesh):
    in_specs = (P("row", "col"), P(None, "row"))
    out_specs = (P("row", "col"), P(None, "row"), P())
    return jax.shard_map(shards, mesh=mesh, in_specs=in_specs, out_specs=out_specs, check_vma=False)
```

```python
import jax
import jax.numpy as jnp
from jax import lax
from jax.experimental import pallas as pl
from jax.experimental.pallas import tpu as pltpu
from jax.sharding import PartitionSpec as P

HI = lax.Precision.HIGHEST
SUB = 8
GROUP = 4
LANES = 128
VMEM = pl.BlockSpec(memory_space=pltpu.VMEM)


def dot(a, b):
    return jnp.dot(a, b, precision=HI, preferred_element_type=jnp.float32)


def dot_t(a, b):
    dims = (((1,), (1,)), ((), ()))
    return lax.dot_general(a, b, dims, precision=HI, preferred_element_type=jnp.float32)


def split(value):
    high = value.astype(jnp.bfloat16)
    rest = value - high.astype(jnp.float32)
    middle = rest.astype(jnp.bfloat16)
    low = (rest - middle.astype(jnp.float32)).astype(jnp.bfloat16)
    return high, middle, low


def outer_sum(left, right):
    a1, a2, a3 = split(jnp.concatenate(left, axis=0))
    b1, b2, b3 = split(jnp.concatenate(right, axis=0))
    a = jnp.concatenate([a1, a1, a2, a1, a2, a3], axis=0)
    b = jnp.concatenate([b1, b2, b1, b3, b2, b1], axis=0)
    dims = (((0,), (0,)), ((), ()))
    return lax.dot_general(a, b, dims, preferred_element_type=jnp.float32)


def factor_tile(blocks):
    shape = (SUB, LANES)
    lane = lax.broadcasted_iota(jnp.int32, shape, 1)
    sub = lax.broadcasted_iota(jnp.int32, shape, 0)
    count = len(blocks)
    blocks = list(blocks)
    upper, inverse, left, right = [], [], [], []
    for b in range(count):
        base = b * SUB
        start = b // GROUP * GROUP
        stop = start + GROUP
        here = blocks[b]
        across = [jnp.broadcast_to(here[:, base + k : base + k + 1], shape) for k in range(SUB)]
        rows = [jnp.broadcast_to(here[k : k + 1, :], shape) for k in range(SUB)]
        s = {}
        for k in range(SUB):
            for i in range(k, SUB):
                s[i, k] = jnp.broadcast_to(across[k][i : i + 1, :], shape)
        rinv, low, u, w = [], {}, [], []
        for k in range(SUB):
            rinv.append(lax.rsqrt(s[k, k]))
            for i in range(k + 1, SUB):
                low[i, k] = s[i, k] * rinv[k]
            for j in range(k + 1, SUB):
                for i in range(j, SUB):
                    s[i, j] = s[i, j] - low[i, k] * low[j, k]
            uk = rows[k]
            wk = jnp.where(lane < base, rows[k], jnp.where(lane == base + k, 1.0, 0.0))
            for m in range(k):
                uk = uk - low[k, m] * u[m]
                wk = wk - low[k, m] * w[m]
            u.append(uk * rinv[k])
            w.append(wk * rinv[k])
        u_block, w_block = u[0], w[0]
        for k in range(1, SUB):
            u_block = jnp.where(sub == k, u[k], u_block)
            w_block = jnp.where(sub == k, w[k], w_block)
        upper.append(jnp.where(lane >= sub + base, u_block, 0.0))
        inverse.append(w_block)
        left.append(u_block)
        right.append(jnp.where(lane < stop * SUB, w_block, u_block))
        if b + 1 == stop:
            if stop < count:
                far = outer_sum(left[start:], right[start:])
                keep = (lane < start * SUB) | (lane >= stop * SUB)
                for i in range(stop, count):
                    blocks[i] = jnp.where(keep, blocks[i], 0.0) - far[i * SUB : (i + 1) * SUB]
            continue
        q = [None] * SUB
        for k in reversed(range(SUB)):
            v = jnp.where(lane < base + SUB, w[k], u[k])
            for m in range(k + 1, SUB):
                v = v - low[m, k] * q[m]
            q[k] = v * rinv[k]
        keep = (lane < base) | (lane >= base + SUB)
        for i in range(b + 1, stop):
            old = blocks[i]
            terms = [
                jnp.broadcast_to(old[:, base + k : base + k + 1], shape) * q[k] for k in range(SUB)
            ]
            while len(terms) > 1:
                terms = [terms[t] + terms[t + 1] for t in range(0, len(terms), 2)]
            blocks[i] = jnp.where(keep, old, 0.0) - terms[0]
    return upper, inverse


def eliminate(corner, below, last, low_ref, inv_ref, diag_ref, tile_here, mid_here):
    square = (LANES, LANES)
    on_diag = lax.broadcasted_iota(jnp.int32, square, 0) == lax.broadcasted_iota(
        jnp.int32, square, 1
    )
    zero = jnp.zeros(square, jnp.float32)
    low_ref[:LANES, LANES:] = zero
    inv_ref[:LANES, LANES:] = zero
    tile_here[...] = corner()

    def step(t, carry):
        tile_rows = pl.ds(pl.multiple_of(t * LANES, LANES), LANES)
        up, inv = factor_tile(
            [tile_here[SUB * i : SUB * (i + 1), :] for i in range(LANES // SUB)]
        )
        up = jnp.concatenate(up, axis=0)
        inv = jnp.concatenate(inv, axis=0)
        diag_ref[pl.ds(t, 1), :] = jnp.sum(jnp.where(on_diag, up, 0.0), axis=0, keepdims=True)
        low_ref[tile_rows, tile_rows] = up.T
        inv_ref[tile_rows, tile_rows] = inv

        @pl.when(t == 0)
        def _():
            left = dot_t(below(), inv)
            low_ref[LANES:, :LANES] = left
            tile_here[...] = last() - dot_t(left, left)
            mid_here[...] = dot(left, inv)

        @pl.when(t == 1)
        def _():
            inv_ref[LANES:, :LANES] = -dot(inv, mid_here[...])

        return carry

    lax.fori_loop(0, 2, step, 0)


def first_kernel(d_ref, both_ref, diag_ref, tile_here, mid_here):
    size = 2 * LANES
    eliminate(
        lambda: d_ref[:LANES, :LANES], lambda: d_ref[LANES:, :LANES],
        lambda: d_ref[LANES:, LANES:size], both_ref.at[:, :size], both_ref.at[:, size:],
        diag_ref, tile_here, mid_here,
    )


def second_kernel(
    d_ref, both0_ref, low_ref, inv_ref, diag_ref, work, low_here, inv_here, tile_here, mid_here
):
    tile = work.shape[0]
    inv0 = both0_ref[:, tile:]
    left = dot_t(d_ref[:, tile : 2 * tile], inv0)
    low_ref[:, :tile] = left
    work[...] = d_ref[:, 2 * tile : 3 * tile] - dot_t(left, left)
    eliminate(
        lambda: work[:LANES, :LANES], lambda: work[LANES:, :LANES], lambda: work[LANES:, LANES:],
        low_here, inv_here, diag_ref, tile_here, mid_here,
    )
    low_ref[:, tile:] = low_here[...]
    inv1 = inv_here[...]
    inv_ref[:, tile:] = inv1
    inv_ref[:, :tile] = -dot(inv1, dot(low_ref[:, :tile], inv0))


def parts_dot(a, b):
    a1, a2, a3 = split(a)
    b1, b2, b3 = split(b)
    a = jnp.concatenate([a1, a1, a2, a1, a2, a3], axis=1)
    b = jnp.concatenate([b1, b2, b1, b3, b2, b1], axis=0)
    return jnp.dot(a, b, preferred_element_type=jnp.float32)


def parts_dot_t(a, b):
    a1, a2, a3 = split(a)
    b1, b2, b3 = split(b)
    a = jnp.concatenate([a1, a1, a2, a1, a2, a3], axis=1)
    b = jnp.concatenate([b1, b2, b1, b3, b2, b1], axis=1)
    dims = (((1,), (1,)), ((), ()))
    return lax.dot_general(a, b, dims, preferred_element_type=jnp.float32)


def finish_kernel(
    ids_ref, panel_ref, ahead_ref, next_ref, rest_ref, wide_ref, both0_ref, diag0_ref, low1_ref, inv1_ref,
    diag1_ref, cov_ref, obs_ref, out_ref, solved_ref, site_ref, rows_here,
):
    tile, wide = cov_ref.shape
    nrhs = obs_ref.shape[0]
    row, col, source = ids_ref[0], ids_ref[1], ids_ref[2]
    inv0 = both0_ref[:, tile:]
    inv10 = inv1_ref[:, :tile]
    inv11 = inv1_ref[:, tile:]

    for place, ref in enumerate([panel_ref, ahead_ref, next_ref, rest_ref]):
        @pl.when(source == place)
        def _(ref=ref):
            rows_here[...] = ref[...]

    obs_both = wide_ref[:, 2 * wide : 2 * wide + 2 * nrhs]
    z0 = parts_dot(inv0, obs_both)[:, :nrhs]
    z1 = parts_dot(inv10, obs_both)[:, :nrhs] + parts_dot(inv11, obs_both)[:, nrhs:]
    quad = jnp.sum(z0 * z0 + z1 * z1, axis=0, keepdims=True)
    logs = jnp.log(diag0_ref[...]) + jnp.log(diag1_ref[...])
    site_ref[...] = -(quad + 2.0 * jnp.sum(logs)) / (4.0 * tile)

    @pl.when(row == 0)
    def _():
        solved_ref[...] = z0.T

    @pl.when(row == 1)
    def _():
        solved_ref[...] = z1.T

    @pl.when(row <= 1)
    def _():
        out_ref[...] = jnp.zeros((tile, wide), jnp.float32)

    @pl.when((row == 0) & (col == 0))
    def _():
        out_ref[:, :tile] = both0_ref[:, :tile]

    @pl.when((row == 1) & (col == 0))
    def _():
        out_ref[...] = low1_ref[...]

    @pl.when(row > 1)
    def _():
        x0 = parts_dot_t(rows_here[:, :tile], inv0)
        x1 = parts_dot_t(rows_here[...], inv1_ref[...])
        solved_ref[...] = obs_ref[...] - (parts_dot(x0, z0) + parts_dot(x1, z1)).T

        @pl.when(col == 0)
        def _():
            out_ref[:, :tile] = x0
            out_ref[:, tile:] = x1

        @pl.when(col > 0)
        def _():
            c0 = wide_ref[:, :wide]
            y0 = parts_dot(inv0, c0)
            y1 = parts_dot(inv10, c0) + parts_dot(inv11, wide_ref[:, wide : 2 * wide])
            out_ref[...] = cov_ref[...] - parts_dot(x0, y0) - parts_dot(x1, y1)


def call(kernel, name, outs, scratch, *args, ids=None):
    flops = 4 * 256**3
    specs = [VMEM] * len(args)
    if ids is not None:
        specs = [pl.BlockSpec(memory_space=pltpu.SMEM)] + specs
        args = (ids,) + args
    return pl.pallas_call(
        kernel,
        out_shape=[jax.ShapeDtypeStruct(shape, jnp.float32) for shape in outs],
        in_specs=specs,
        out_specs=[VMEM] * len(outs),
        scratch_shapes=[pltpu.VMEM(shape, jnp.float32) for shape in scratch],
        compiler_params=pltpu.CompilerParams(vmem_limit_bytes=16 * 1024 * 1024),
        cost_estimate=pl.CostEstimate(flops=flops, bytes_accessed=40 * 2**20, transcendentals=0),
        name=name,
    )(*args)


def send(value, hop, holders, extent):
    pairs = [(z, (z + hop) % extent) for z in holders]
    return lax.ppermute(value, "col", pairs), [target for _, target in pairs]


def pick(value, moved, targets, position):
    is_new = jnp.zeros((), bool)
    for target in targets:
        is_new = is_new | (position == target)
    return jnp.where(is_new, moved, value)


def spread_step(value, hops, holders, extent, position):
    sent = [send(value, hop, holders, extent) for hop in hops]
    reached = set(holders)
    for moved, targets in sent:
        value = pick(value, moved, targets, position)
        reached |= set(targets)
    return value, sorted(reached)


def shards(covariance, observations):
    tile, wide = covariance.shape
    nrhs = observations.shape[0]
    rows = lax.axis_size("row")
    cols = lax.axis_size("col")
    row = lax.axis_index("row")
    col = lax.axis_index("col")
    part = tile // rows

    def exchange(value):
        return lax.all_to_all(value, "row", split_axis=0, concat_axis=0, tiled=True)

    with jax.named_scope("scatter"):
        got = exchange(covariance.reshape(rows, part, wide))
        first, second = got[0], got[1]
        obs_parts = jnp.pad(observations.T, ((0, 0), (0, LANES - nrhs))).reshape(rows, part, LANES)

    with jax.named_scope("diag"):
        piece = jnp.concatenate([first[:, :tile], second], axis=1)
        near, reached = send(piece, 5, [0], cols)
        piece, near, reached = pick(piece, near, reached, col), piece, [0] + reached
        back, backs = send(piece, -2, reached, cols)
        ahead, aheads = send(piece, 2, reached, cols)
        near, piece = lax.optimization_barrier((near, piece))
        far, fars = send(near, -5, [0], cols)
        piece = pick(piece, far, fars, col)
        far_back, far_backs = send(piece, -2, fars, cols)
        far_ahead, far_aheads = send(piece, 2, fars, cols)
        piece = pick(pick(piece, back, backs, col), ahead, aheads, col)
        piece = pick(pick(piece, far_back, far_backs, col), far_ahead, far_aheads, col)
        last = [z for z in range(cols) if z in reached + backs + aheads + fars + far_backs + far_aheads]
        last = [z for z in last if (z + 1) % cols not in last]
        piece, _ = spread_step(piece, (1,), last, cols, col)
        panel, piece = lax.optimization_barrier((covariance, piece))
        sent = jnp.broadcast_to(piece[None], (rows,) + piece.shape)
        whole = exchange(jnp.concatenate([sent, obs_parts], axis=2))
        diag = whole.reshape(tile, -1)

    with jax.named_scope("columns"):
        start = 3 * tile
        col_piece = jnp.concatenate(
            [first, second, whole[0, :, start : start + nrhs], whole[1, :, start : start + nrhs]],
            axis=1,
        )
        columns = exchange(jnp.broadcast_to(col_piece[None], (rows,) + col_piece.shape))
        columns = columns.reshape(tile, -1)

    with jax.named_scope("rowpanel"):
        panel, holders = spread_step(panel, (5, -5), [0], cols, col)
        ahead = send(panel, 2, holders, cols)
        panel, holders = spread_step(panel, (-2,), holders, cols, col)

    square = (LANES, LANES)
    both0, diag0 = call(
        first_kernel, "factor_first", [(tile, wide), (tile // LANES, LANES)], [square] * 2, diag
    )
    both0, panel, columns = lax.optimization_barrier((both0, panel, columns))
    with jax.named_scope("rowpanel"):
        covered = set(holders) | set(ahead[1])
        after = [z for z in holders if (z + 1) % cols not in covered]
        sends = [ahead, send(panel, 1, after, cols)]
        covered |= set(sends[1][1])
        rest = [z for z in holders if (z - 1) % cols not in covered]
        sends.append(send(panel, -1, rest, cols))
    low1, inv1, diag1 = call(
        second_kernel, "factor_second", [(tile, wide), (tile, wide), (tile // LANES, LANES)],
        [(tile, tile)] * 3 + [square] * 2, diag, both0,
    )

    source = jnp.zeros((), jnp.int32)
    for place, (_, targets) in enumerate(sends):
        for target in targets:
            source = jnp.where(col == target, place + 1, source)
    ids = jnp.stack([row, col, source])
    factored, solved, site = call(
        finish_kernel, "finish", [(tile, wide), (nrhs, tile), (1, nrhs)], [(tile, wide)],
        panel, *[moved for moved, _ in sends], columns, both0, diag0, low1, inv1, diag1, covariance, observations,
        ids=ids,
    )
    return factored, solved, site.reshape(nrhs)


def solution(mesh):
    in_specs = (P("row", "col"), P(None, "row"))
    out_specs = (P("row", "col"), P(None, "row"), P())
    return jax.shard_map(shards, mesh=mesh, in_specs=in_specs, out_specs=out_specs, check_vma=False)
```
